128 devices in a mesh: row: 8 (over x, y_hi), col: 4 (over y_lo, core), depth: 4 (over z).
Axes of the slice: x: 4, y: 4 (y_hi: 2, y_lo: 2; y = y_hi * 2 + y_lo), z: 4, core: 2. Of those that a mesh axis runs over, the one named last changes fastest.
Arguments:
- tokens: bfloat16 [768, 8192], P(('depth', 'col'), 'row'), may hold values from -6 to 6
- gate_weight: bfloat16 [8192, 14336], P('row', ('col', 'depth')), may hold values from -0.0625 to 0.0625
- up_weight: bfloat16 [8192, 14336], P('row', ('col', 'depth')), may hold values from -0.0625 to 0.0625
- down_weight: bfloat16 [14336, 8192], P(('col', 'depth'), 'row'), may hold values from -0.046875 to 0.046875
- cotangent: bfloat16 [768, 8192], P(('depth', 'col'), 'row'), may hold values from -0.86328125 to 0.86328125
Outputs:
- mixed: float32 [768, 8192], P(('depth', 'col'), 'row')
- token_grad: float32 [768, 8192], P(('depth', 'col'), 'row')
- gate_weight_grad: float32 [8192, 14336], P('row', ('col', 'depth'))
- up_weight_grad: float32 [8192, 14336], P('row', ('col', 'depth'))
- down_weight_grad: float32 [14336, 8192], P(('col', 'depth'), 'row')
The draws below stay inside these ranges and needn't reach their ends.
All inputs are finite; a program needn't handle non-finite values.
Results may differ from the reference program's by a relative error of at most 0.012.
Values may be sent and summed in bfloat16 or wider, within the bound.
A program may use at most 192 MiB of HBM per device.

```python
import jax
import jax.numpy as jnp
from jax import lax

D = 8192
FF = 14336
TOK_L = 192
TOKENS = 768
N_DEPTH = 4


def block_levels(rng, dims, cuts, smallest, high):
    def one(dim, shards_of):
        draws = jax.random.uniform(jax.random.fold_in(jax.random.fold_in(rng, 6), dim), (shards_of,), jnp.float32, smallest / len(cuts), high / len(cuts))
        return jnp.repeat(jnp.exp(draws), dims[dim] // shards_of).reshape((-1,) + (1,) * (len(dims) - dim - 1))

    gain = one(*cuts[0])
    for cut in cuts[1:]:
        gain = gain * one(*cut)
    return gain


def normal_values(key, extent, spread, bound, pieces=(), held_as=jnp.bfloat16):
    factor_of = block_levels(key, extent, pieces, -0.22, 0.18) if pieces else 1.0
    result = jax.random.normal(key, extent, jnp.float32) * spread * factor_of
    return jnp.minimum(jnp.maximum(result, -bound), bound).astype(held_as)


def setup_inputs(seed: int = 0) -> dict:
    seeds = jax.random.split(jax.random.key(seed), 6)
    tokens = normal_values(seeds[0], (TOKENS, D), 1.0, 6.0, ((0, 16), (1, 8)))
    gate_weight = normal_values(seeds[1], (D, FF), D ** -0.5, 0.0625, ((0, 8), (1, 16)))
    up_weight = normal_values(seeds[2], (D, FF), D ** -0.5, 0.0625, ((0, 8), (1, 16)))
    down_weight = normal_values(seeds[3], (FF, D), FF ** -0.5, 0.046875, ((0, 16), (1, 8)))
    cotangent = normal_values(seeds[4], (TOKENS, D), (4.0 / TOKENS ** 0.5), 0.86328125, ((0, 16), (1, 8)))
    return dict(tokens=tokens, gate_weight=gate_weight, up_weight=up_weight, down_weight=down_weight, cotangent=cotangent)


def swish_parts(gate):
    sigma_gate = jax.nn.sigmoid(gate)
    return gate * sigma_gate, sigma_gate


def rounded_sum(total, left_side, right_side):
    partial_term = jnp.dot(left_side.T, right_side, preferred_element_type=jnp.float32).astype(jnp.bfloat16)
    return total + lax.optimization_barrier(partial_term).astype(jnp.float32)


def reference(tokens, gate_weight, up_weight, down_weight, cotangent):
    gate = jnp.dot(tokens, gate_weight, preferred_element_type=jnp.float32)
    up_full = jnp.dot(tokens, up_weight, preferred_element_type=jnp.float32)
    activated, sigma_gate = swish_parts(gate)
    hidden = (activated * up_full).astype(jnp.bfloat16)
    mixed = jnp.dot(hidden, down_weight, preferred_element_type=jnp.float32)
    hidden_grad = jnp.dot(cotangent, down_weight.T, preferred_element_type=jnp.float32)
    gate_grad = (hidden_grad * up_full * sigma_gate * (1.0 + gate * (1.0 - sigma_gate))).astype(jnp.bfloat16)
    up_grad = (hidden_grad * activated).astype(jnp.bfloat16)
    token_grad = (jnp.dot(gate_grad, gate_weight.T, preferred_element_type=jnp.float32)
                  + jnp.dot(up_grad, up_weight.T, preferred_element_type=jnp.float32))
    gate_total = jnp.zeros((D, FF), jnp.float32)
    up_total = jnp.zeros((D, FF), jnp.float32)
    down_total = jnp.zeros((FF, D), jnp.float32)
    for layer_index in range(N_DEPTH):
        first_row = layer_index * TOK_L
        last_row = first_row + TOK_L
        tokens_layer = tokens[first_row:last_row]
        gate_total = rounded_sum(gate_total, tokens_layer, gate_grad[first_row:last_row])
        up_total = rounded_sum(up_total, tokens_layer, up_grad[first_row:last_row])
        down_total = rounded_sum(down_total, hidden[first_row:last_row], cotangent[first_row:last_row])
    return (mixed, token_grad, gate_total, up_total, down_total)
```

```python
import functools

import jax
import jax.numpy as jnp
from jax import lax
from jax.experimental import pallas as pl
from jax.experimental.pallas import tpu as pltpu
from jax.sharding import PartitionSpec as P

MESH = pl.DeviceIdType.MESH
BF = jnp.bfloat16
F32 = jnp.float32
OFFSETS = (0, 2, 1, 3)
B = 48
D = 1024
F = 896
CUT = 512


def dot(a, b):
    return jnp.dot(a, b, preferred_element_type=F32)


def dot_t(a, b):
    return lax.dot_general(a, b, (((1,), (1,)), ((), ())), preferred_element_type=F32)


def kernel(tok_in, cot_in, gw_in, uw_in, dw_in,
           mixed_out, tg_out, buf_out, all_out,
           buf, gw, uw, dw, part0, part1, r0y, s0, r0x, r1x, s1, r1y, all0, all1, pk, sk, ps, pr,
           w_sem, l_sem, o_sem, p1s, p1r, fs, fr,
           s0y_s, s0y_r, s0x_s, s0x_r, s1x_s, s1x_r, s1y_s, s1y_r,
           g0x_s, g0x_r, g0y_s, g0y_r, g1y_s, g1y_r, g1x_s, g1x_r,
           ks, kr, p4s, p4r):
    row, col, z = lax.axis_index("row"), lax.axis_index("col"), lax.axis_index("depth")
    x, yh = row // 2, row % 2
    yl, k = col // 2, col % 2

    sibling = (row, yl * 2 + (1 - k), z)
    y_peer = (x * 2 + (1 - yh), col, z)

    def x_at(dx):
        return (x + dx) % 4

    def x_peer(dx):
        return (x_at(dx) * 2 + yh, col, z)

    def plane_peer(dz, dyl):
        return (row, ((yl + dyl) % 2) * 2 + k, (z + dz) % 4)

    others = [(t, dyl) for t in range(4) for dyl in range(2) if (t, dyl) != (0, 0)]
    sends = []

    def remote(src, dst, ssem, rsem, dev):
        cp = pltpu.make_async_remote_copy(src_ref=src, dst_ref=dst, send_sem=ssem, recv_sem=rsem,
                                          device_id=dev, device_id_type=MESH)
        cp.start()
        sends.append(cp)
        return cp

    weights = [pltpu.make_async_copy(a, b, w_sem.at[i])
               for i, (a, b) in enumerate(((gw_in, gw), (uw_in, uw), (dw_in, dw)))]
    own = [pltpu.make_async_copy(a, buf.at[i, col], l_sem.at[i]) for i, a in enumerate((tok_in, cot_in))]
    for cp in own + weights:
        cp.start()

    barrier = pltpu.get_barrier_semaphore()
    peers = [sibling, y_peer] + [x_peer(dx) for dx in (1, 2, 3)]
    peers += [plane_peer(OFFSETS[t], dyl) for t, dyl in others]
    for dev in peers:
        pl.semaphore_signal(barrier, inc=1, device_id=dev, device_id_type=MESH)
    pl.semaphore_wait(barrier, len(peers))
    for cp in own:
        cp.wait()

    arrived, handed = {}, {}

    def share(t, dyl):
        i = t * 2 + dyl
        arrived[i] = remote(buf.at[:, col], buf.at[:, t * 4 + col], p1s.at[i], p1r.at[i],
                            plane_peer(-OFFSETS[t], dyl))

    def hand_on(t, dyl):
        i = t * 2 + dyl
        slot = t * 4 + ((yl + dyl) % 2) * 2 + k
        handed[i] = remote(buf.at[:, slot], buf.at[:, slot], fs.at[i], fr.at[i], sibling)

    def take(half):
        for t in (2 * half, 2 * half + 1):
            for dyl in range(2):
                if t or dyl:
                    arrived[t * 2 + dyl].wait_recv()
                    hand_on(t, dyl)

    def ready(half):
        for i in range(4 * half, 4 * half + 4):
            handed[i].wait_recv()

    for t, dyl in ((0, 1), (1, 0), (1, 1)):
        share(t, dyl)
    hand_on(0, 0)

    def partial(half, dst, lo, width):
        rows = [buf[a, 8 * half:8 * half + 8].reshape(8 * B, D) for a in range(2)]
        cols = slice(lo, lo + width)
        for i, value in enumerate((lambda: dot(rows[0], gw[:, cols]), lambda: dot(rows[0], uw[:, cols]),
                                   lambda: dot_t(rows[1], dw[cols, :]))):
            dst[half, i] = value().astype(BF).reshape(8, B, width)

    rs0y, rs1x, rs0x, rs1y = {}, {}, {}, {}

    def send0y(h):
        rs0y[h] = remote(part0.at[h, :, pl.ds((1 - yh) * 4, 4)], r0y.at[h], s0y_s.at[h], s0y_r.at[h], y_peer)

    def send1x(h):
        rs1x[h] = [remote(part1.at[h, :, pl.ds(x_at(dx) * 2, 2)], r1x.at[h, dx - 1],
                          s1x_s.at[h, dx - 1], s1x_r.at[h, dx - 1], x_peer(dx)) for dx in (1, 2, 3)]

    def send0x(h):
        rs0y[h].wait_recv()
        s0[h] = (part0[h, :, pl.ds(yh * 4, 4)].astype(F32) + r0y[h].astype(F32)).astype(BF)
        rs0x[h] = [remote(s0.at[h, :, x_at(dx)], r0x.at[h, dx - 1],
                          s0x_s.at[h, dx - 1], s0x_r.at[h, dx - 1], x_peer(dx)) for dx in (1, 2, 3)]

    def send1y(h):
        for cp in rs1x[h]:
            cp.wait_recv()
        total = part1[h, :, pl.ds(x * 2, 2)].astype(F32)
        for i in range(3):
            total = total + r1x[h, i].astype(F32)
        s1[h] = total.astype(BF)
        rs1y[h] = remote(s1.at[h, :, 1 - yh], r1y.at[h], s1y_s.at[h], s1y_r.at[h], y_peer)

    def activate(total, dst, slot):
        gate, up, hidden_grad = total[0], total[1], total[2]
        sigma = jax.nn.sigmoid(gate)
        activated = gate * sigma
        dst[0, slot] = (activated * up).astype(BF)
        dst[1, slot] = (hidden_grad * up * sigma * (1.0 + gate * (1.0 - sigma))).astype(BF)
        dst[2, slot] = (hidden_grad * activated).astype(BF)

    ag0x, ag0y, ag1y, ag1x = {}, {}, {}, {}

    def gather0x(h):
        for cp in rs0x[h]:
            cp.wait_recv()
        total = s0[h, :, x].astype(F32)
        for i in range(3):
            total = total + r0x[h, i].astype(F32)
        slot = h * 8 + yh * 4 + x
        activate(total, all0, slot)
        ag0x[h] = [remote(all0.at[:, slot], all0.at[:, slot], g0x_s.at[h, dx - 1], g0x_r.at[h, dx - 1], x_peer(dx))
                   for dx in (1, 2, 3)]

    def gather1y(h):
        rs1y[h].wait_recv()
        total = s1[h, :, yh].astype(F32) + r1y[h].astype(F32)
        slot = h * 8 + x * 2 + yh
        activate(total, all1, slot)
        ag1y[h] = remote(all1.at[:, slot], all1.at[:, slot], g1y_s.at[h], g1y_r.at[h], y_peer)

    def gather0y(h):
        for cp in ag0x[h]:
            cp.wait_recv()
        slots = pl.ds(h * 8 + yh * 4, 4)
        ag0y[h] = remote(all0.at[:, slots], all0.at[:, slots], g0y_s.at[h], g0y_r.at[h], y_peer)

    def gather1x(h):
        ag1y[h].wait_recv()
        slots = pl.ds(h * 8 + x * 2, 2)
        ag1x[h] = [remote(all1.at[:, slots], all1.at[:, slots], g1x_s.at[h, dx - 1], g1x_r.at[h, dx - 1], x_peer(dx))
                   for dx in (1, 2, 3)]

    pair = {}

    def outputs(h):
        ag0y[h].wait_recv()
        for cp in ag1x[h]:
            cp.wait_recv()
        rows = slice(8 * h, 8 * h + 8)
        left = [(all0[i, rows].reshape(8 * B, CUT), all1[i, rows].reshape(8 * B, F - CUT)) for i in range(3)]
        for n in range(2):
            cols = slice(n * 512, n * 512 + 512)
            mixed = dot(left[0][0], dw[:CUT, cols]) + dot(left[0][1], dw[CUT:, cols])
            grad = (dot_t(left[1][0], gw[cols, :CUT]) + dot_t(left[1][1], gw[cols, CUT:])
                    + dot_t(left[2][0], uw[cols, :CUT]) + dot_t(left[2][1], uw[cols, CUT:]))
            for a, value in enumerate((mixed, grad)):
                value = value.astype(BF).reshape(4, 2, B, 512)
                for core in range(2):
                    pk[core, a, 4 * h:4 * h + 4, :, cols] = value[:, core]
        half = pl.ds(4 * h, 4)
        pair[h] = remote(pk.at[1 - k, :, half], sk.at[:, half], ks.at[h], kr.at[h], sibling)

    spread = {}

    def reduce(h):
        pair[h].wait_recv()
        half = slice(4 * h, 4 * h + 4)
        ps[:, half] = (pk[k, :, half].astype(F32) + sk[:, half].astype(F32)).astype(BF)
        for t in (2 * h, 2 * h + 1):
            for dyl in range(2):
                if t or dyl:
                    i = t * 2 + dyl
                    spread[i] = remote(ps.at[:, t * 2 + (yl + dyl) % 2], pr.at[i], p4s.at[i], p4r.at[i],
                                       plane_peer(OFFSETS[t], dyl))

    take(0)
    for t, dyl in ((2, 0), (3, 0), (2, 1), (3, 1)):
        share(t, dyl)
    for cp in weights:
        cp.wait()
    ready(0)
    partial(0, part0, 0, CUT)
    send0y(0)
    partial(0, part1, CUT, F - CUT)
    send1x(0)
    take(1)
    ready(1)
    partial(1, part0, 0, CUT)
    send0y(1)
    partial(1, part1, CUT, F - CUT)
    send1x(1)
    send1y(0)
    send0x(0)
    gather1y(0)
    gather0x(0)
    gather1x(0)
    gather0y(0)
    send1y(1)
    send0x(1)
    gather1y(1)
    gather0x(1)
    gather1x(1)
    gather0y(1)
    outputs(0)
    reduce(0)
    outputs(1)
    reduce(1)

    results = [pltpu.make_async_copy(buf, buf_out, o_sem.at[0]),
               pltpu.make_async_copy(all0, all_out.at[:, :, :, pl.ds(0, CUT)], o_sem.at[1]),
               pltpu.make_async_copy(all1, all_out.at[:, :, :, pl.ds(CUT, F - CUT)], o_sem.at[2])]
    for cp in results:
        cp.start()

    total = ps[:, yl].astype(F32)
    for t, dyl in others:
        i = t * 2 + dyl
        spread[i].wait_recv()
        total = total + pr[i].astype(F32)
    mixed_out[...] = total[0]
    tg_out[...] = total[1]
    for cp in sends:
        cp.wait_send()
    for cp in results:
        cp.wait()


def body(tokens, gate_weight, up_weight, down_weight, cotangent):
    dma = pltpu.SemaphoreType.DMA
    vmem = lambda *shape: pltpu.VMEM(shape, BF)
    whole = pl.BlockSpec(memory_space=pl.ANY)
    G = F - CUT
    mixed, token_grad, rows, hidden = pl.pallas_call(
        kernel,
        out_shape=(
            jax.ShapeDtypeStruct((B, D), F32),
            jax.ShapeDtypeStruct((B, D), F32),
            jax.ShapeDtypeStruct((2, 16, B, D), BF),
            jax.ShapeDtypeStruct((3, 16, B, F), BF),
        ),
        in_specs=[whole] * 5,
        out_specs=(pl.BlockSpec(memory_space=pltpu.VMEM),) * 2 + (whole,) * 2,
        scratch_shapes=[
            vmem(2, 16, B, D), vmem(D, F), vmem(D, F), vmem(F, D),
            vmem(2, 3, 8, B, CUT), vmem(2, 3, 8, B, G),
            vmem(2, 3, 4, B, CUT), vmem(2, 3, 4, B, CUT), vmem(2, 3, 3, B, CUT),
            vmem(2, 3, 3, 2, B, G), vmem(2, 3, 2, B, G), vmem(2, 3, B, G),
            vmem(3, 16, B, CUT), vmem(3, 16, B, G),
            vmem(2, 2, 8, B, D), vmem(2, 8, B, D), vmem(2, 8, B, D), vmem(8, 2, B, D),
            dma((3,)), dma((2,)), dma((3,)), dma((8,)), dma((8,)), dma((8,)), dma((8,)),
            dma((2,)), dma((2,)), dma((2, 3)), dma((2, 3)), dma((2, 3)), dma((2, 3)), dma((2,)), dma((2,)),
            dma((2, 3)), dma((2, 3)), dma((2,)), dma((2,)), dma((2,)), dma((2,)), dma((2, 3)), dma((2, 3)),
            dma((2,)), dma((2,)), dma((8,)), dma((8,)),
        ],
        compiler_params=pltpu.CompilerParams(
            collective_id=0, has_side_effects=True, vmem_limit_bytes=60 * 2**20
        ),
    )(tokens, cotangent, gate_weight, up_weight, down_weight)
    tokens_all, cotangent_all = rows[0].reshape(16 * B, D), rows[1].reshape(16 * B, D)
    hidden_all, gate_grad, up_grad = (hidden[i].reshape(16 * B, F) for i in range(3))

    def over_tokens(left, right):
        return lax.dot_general(left, right, (((0,), (0,)), ((), ())), preferred_element_type=F32)

    return (mixed, token_grad, over_tokens(tokens_all, gate_grad), over_tokens(tokens_all, up_grad),
            over_tokens(hidden_all, cotangent_all))


def solution(mesh):
    placed = (
        P(("depth", "col"), "row"),
        P("row", ("col", "depth")),
        P("row", ("col", "depth")),
        P(("col", "depth"), "row"),
        P(("depth", "col"), "row"),
    )
    return jax.shard_map(
        body,
        mesh=mesh,
        in_specs=placed,
        out_specs=(
            P(("depth", "col"), "row"),
            P(("depth", "col"), "row"),
            P("row", ("col", "depth")),
            P("row", ("col", "depth")),
            P(("col", "depth"), "row"),
        ),
        check_vma=False,
    )
```

```python
import functools

import jax
import jax.numpy as jnp
from jax import lax
from jax.experimental import pallas as pl
from jax.experimental.pallas import tpu as pltpu
from jax.sharding import PartitionSpec as P

MESH = pl.DeviceIdType.MESH
BF = jnp.bfloat16
F32 = jnp.float32
OFFSETS = (0, 2, 1, 3)
B = 48
D = 1024
F = 896
CUT = 512
G = F - CUT
PIECE = 256


def dot(a, b):
    return jnp.dot(a, b, preferred_element_type=F32)


def dot_t(a, b):
    return lax.dot_general(a, b, (((1,), (1,)), ((), ())), preferred_element_type=F32)


def dot_rows(a, b):
    return lax.dot_general(a, b, (((0,), (0,)), ((), ())), preferred_element_type=F32)


def kernel(tok_in, cot_in, gw_in, uw_in, dw_in,
           mixed_out, tg_out, gate_out, up_out, down_out,
           buf, gw, uw, dw, part0, part1, xa, xd, xc, s0, r0y, y1, s1, ya, yb, all0, all1,
           pk, sk, ps, pz, pq, py, pr, gate_acc, up_acc, down_acc,
           w_sem, l_sem, p1s, p1r, fs, fr,
           xa_s, xa_r, xd_s, xd_r, xc_s, xc_r, r0y_s, r0y_r, y1_s, y1_r, ya_s, ya_r, yb_s, yb_r,
           g0y_s, g0y_r, g0x_s, g0x_r, g0f_s, g0f_r, g1x_s, g1x_r, g1f_s, g1f_r, g1y_s, g1y_r,
           ks, kr, p4s, p4r):
    row, col, z = lax.axis_index("row"), lax.axis_index("col"), lax.axis_index("depth")
    x, yh = row // 2, row % 2
    yl, k = col // 2, col % 2
    turn = 1 - 2 * k
    mate = (1 - yl) * 2 + k

    sibling = (row, yl * 2 + (1 - k), z)
    y_peer = (x * 2 + (1 - yh), col, z)
    lo_peer = (row, mate, z)

    def x_at(dx):
        return (x + dx + 8) % 4

    def x_peer(dx):
        return (x_at(dx) * 2 + yh, col, z)

    def plane_peer(dz, dyl):
        return (row, ((yl + dyl) % 2) * 2 + k, (z + dz) % 4)

    others = [(t, dyl) for t in range(4) for dyl in range(2) if (t, dyl) != (0, 0)]
    sends = []

    def remote(src, dst, ssem, rsem, dev):
        cp = pltpu.make_async_remote_copy(src_ref=src, dst_ref=dst, send_sem=ssem, recv_sem=rsem,
                                          device_id=dev, device_id_type=MESH)
        cp.start()
        sends.append(cp)
        return cp

    weights = [pltpu.make_async_copy(a, b, w_sem.at[i])
               for i, (a, b) in enumerate(((gw_in, gw), (uw_in, uw), (dw_in, dw)))]
    own = [pltpu.make_async_copy(a, buf.at[i, col], l_sem.at[i]) for i, a in enumerate((tok_in, cot_in))]
    for cp in own + weights:
        cp.start()

    barrier = pltpu.get_barrier_semaphore()
    peers = [sibling, y_peer] + [x_peer(dx) for dx in (1, 3)]
    peers += [plane_peer(OFFSETS[t], dyl) for t, dyl in others]
    for dev in peers:
        pl.semaphore_signal(barrier, inc=1, device_id=dev, device_id_type=MESH)
    pl.semaphore_wait(barrier, len(peers))

    moved, handed = {}, {}

    def share(name, a, i, src, dst, dev):
        moved[name, a] = remote(buf.at[a, src], buf.at[a, dst], p1s.at[a, i], p1r.at[a, i], dev)

    def hand_on(a, i, slot):
        handed[a, i] = remote(buf.at[a, slot], buf.at[a, slot], fs.at[a, i], fr.at[a, i], sibling)

    def spread_first():
        for a in range(2):
            own[a].wait()
            share("lo", a, 0, col, col, lo_peer)
            share("far", a, 1, col, 4 + col, plane_peer(2, 0))
            hand_on(a, 0, col)
        for a in range(2):
            moved["lo", a].wait_recv()
            hand_on(a, 1, mate)
            moved["far", a].wait_recv()
            share("far_lo", a, 6, 4 + col, 4 + col, lo_peer)
            hand_on(a, 2, 4 + col)
            for i, (t, slot) in enumerate(((2, col), (3, col), (2, mate), (3, mate))):
                share((t, i // 2), a, 2 + i, slot, 4 * t + slot, plane_peer(-OFFSETS[t], 0))

    def spread_last(a):
        moved["far_lo", a].wait_recv()
        hand_on(a, 3, 4 + mate)

    def spread_second(a):
        for i, slot in enumerate((col, mate)):
            for t in (2, 3):
                moved[(t, i), a].wait_recv()
                hand_on(a, 2 * t + i, 4 * t + slot)

    def ready(h, a):
        for i in range(4 * h, 4 * h + 4):
            handed[a, i].wait_recv()

    def tokens_part(h, dst, lo, width):
        rows = buf[0, 8 * h:8 * h + 8].reshape(8 * B, D)
        for i, weight in enumerate((gw, uw)):
            dst[h, i] = dot(rows, weight[:, lo:lo + width]).astype(BF).reshape(8, B, width)

    def cotangent_part(h, dst, lo, width):
        rows = buf[1, 8 * h:8 * h + 8].reshape(8 * B, D)
        dst[h, 2] = dot_t(rows, dw[lo:lo + width, :]).astype(BF).reshape(8, B, width)

    def activate(total, dst, slot):
        gate, up, hidden_grad = total[0], total[1], total[2]
        sigma = jax.nn.sigmoid(gate)
        activated = gate * sigma
        dst[0, slot] = (activated * up).astype(BF)
        dst[1, slot] = (hidden_grad * up * sigma * (1.0 + gate * (1.0 - sigma))).astype(BF)
        dst[2, slot] = (hidden_grad * activated).astype(BF)

    cxa, cxd, cxc, cr0 = {}, {}, {}, {}

    def x_tokens(h):
        tokens_part(h, part0, 0, CUT)

    def x_first(h):
        cotangent_part(h, part0, 0, CUT)
        cxa[h] = [remote(part0.at[h, :, x_at(2) * 2 + i], xa.at[h, i], xa_s.at[h, i], xa_r.at[h, i], x_peer(1 - 2 * i))
                  for i in range(2)]
        cxd[h] = [remote(part0.at[h, :, x_at(1 - 2 * i) * 2 + 1 - i], xd.at[h, i], xd_s.at[h, i], xd_r.at[h, i],
                         x_peer(1 - 2 * i)) for i in range(2)]

    def x_second(h):
        cxc[h] = []
        for i in range(2):
            cxa[h][i].wait_recv()
            xa[h, i] = (xa[h, i].astype(F32) + part0[h, :, x_at(1 - 2 * i) * 2 + i].astype(F32)).astype(BF)
            cxc[h].append(remote(xa.at[h, i], xc.at[h, i], xc_s.at[h, i], xc_r.at[h, i], x_peer(1 - 2 * i)))

    def x_third(h):
        for cp in cxd[h] + cxc[h]:
            cp.wait_recv()
        for i in range(2):
            s0[h, :, i] = (part0[h, :, x * 2 + i].astype(F32) + xd[h, 1 - i].astype(F32)
                           + xc[h, i].astype(F32)).astype(BF)
        cr0[h] = remote(s0.at[h, :, 1 - yh], r0y.at[h], r0y_s.at[h], r0y_r.at[h], y_peer)

    cy1, cya, cyb = {}, {}, {}

    def y_first(h):
        tokens_part(h, part1, CUT, G)
        cotangent_part(h, part1, CUT, G)
        cy1[h] = {j: remote(part1.at[h, :, (1 - yh) * 4 + x_at(turn * j)], y1.at[h, j], y1_s.at[h, j], y1_r.at[h, j],
                            y_peer) for j in (2, 1, 3, 0)}
        cya[h], cyb[h] = {}, {}

    def lap(h, kind, src, ways):
        if "a" in ways:
            cya[h][kind] = remote(src.at[:, :, pl.ds(0, PIECE)], ya.at[h, kind], ya_s.at[h, kind], ya_r.at[h, kind],
                                  x_peer(turn if kind != 1 else -turn))
        if "b" in ways:
            cyb[h][kind] = remote(src.at[:, :, pl.ds(PIECE, G - PIECE)], yb.at[h, kind], yb_s.at[h, kind],
                                  yb_r.at[h, kind], x_peer(-turn if kind != 1 else turn))

    def y_second(h):
        for j in (2, 1, 3, 0):
            cy1[h][j].wait_recv()
            s1[h, j] = (part1[h, :, yh * 4 + x_at(turn * j)].astype(F32) + y1[h, j].astype(F32)).astype(BF)
            if j == 2:
                lap(h, 0, s1.at[h, 2], "ab")
            elif j == 1:
                lap(h, 1, s1.at[h, 1], "b")
            elif j == 3:
                lap(h, 1, s1.at[h, 3], "a")

    def y_third(h):
        cya[h][0].wait_recv()
        s1[h, 1, :, :, :PIECE] = (s1[h, 1, :, :, :PIECE].astype(F32) + ya[h, 0].astype(F32)).astype(BF)
        lap(h, 2, s1.at[h, 1], "a")
        cyb[h][0].wait_recv()
        s1[h, 3, :, :, PIECE:] = (s1[h, 3, :, :, PIECE:].astype(F32) + yb[h, 0].astype(F32)).astype(BF)
        lap(h, 2, s1.at[h, 3], "b")

    cg0y, cg0x, cg0f, cg1x, cg1f, cg1y = {}, {}, {}, {}, {}, {}

    def gather0(h, slot, kind):
        for i in range(2):
            cg0x[h, i, kind] = remote(all0.at[:, slot], all0.at[:, slot], g0x_s.at[h, i, kind], g0x_r.at[h, i, kind],
                                      x_peer(1 - 2 * i))

    def x_gather(h):
        cr0[h].wait_recv()
        slot = h * 8 + x * 2 + yh
        activate(s0[h, :, yh].astype(F32) + r0y[h].astype(F32), all0, slot)
        cg0y[h] = remote(all0.at[:, slot], all0.at[:, slot], g0y_s.at[h], g0y_r.at[h], y_peer)
        gather0(h, slot, 0)

    def x_gather_second(h):
        cg0y[h].wait_recv()
        gather0(h, h * 8 + x * 2 + 1 - yh, 1)

    def x_forward(h):
        for i, slot in enumerate((h * 8 + x_at(-1) * 2 + yh, h * 8 + x_at(1) * 2 + 1 - yh)):
            cg0x[h, i, i].wait_recv()
            cg0f[h, i] = remote(all0.at[:, slot], all0.at[:, slot], g0f_s.at[h, i], g0f_r.at[h, i], x_peer(1 - 2 * i))

    def x_done(h):
        for cp in (cg0x[h, 0, 1], cg0x[h, 1, 0], cg0f[h, 0], cg0f[h, 1]):
            cp.wait_recv()

    def to_y(h, j, slot):
        cg1y[h, j] = remote(all1.at[:, slot], all1.at[:, slot], g1y_s.at[h, j], g1y_r.at[h, j], y_peer)

    def y_gather(h):
        for cp in (cya[h][1], cya[h][2], cyb[h][1], cyb[h][2]):
            cp.wait_recv()
        mine = s1[h, 0].astype(F32)
        left = mine[:, :, :PIECE] + ya[h, 1].astype(F32) + ya[h, 2].astype(F32)
        right = mine[:, :, PIECE:] + yb[h, 1].astype(F32) + yb[h, 2].astype(F32)
        slot = h * 8 + yh * 4 + x
        activate(jnp.concatenate([left, right], axis=2), all1, slot)
        for i in range(2):
            cg1x[h, i] = remote(all1.at[:, slot], all1.at[:, slot], g1x_s.at[h, i], g1x_r.at[h, i],
                                x_peer(turn * (1 - 2 * i)))
        to_y(h, 0, slot)

    def y_forward(h):
        for i, (lo, width) in enumerate(((0, PIECE), (PIECE, G - PIECE))):
            slot = h * 8 + yh * 4 + x_at(turn * (2 * i - 1))
            cg1x[h, i].wait_recv()
            piece = all1.at[:, slot, :, pl.ds(lo, width)]
            cg1f[h, i] = remote(piece, piece, g1f_s.at[h, i], g1f_r.at[h, i], x_peer(turn * (1 - 2 * i)))
            to_y(h, 3 - 2 * i, slot)

    def y_forward_last(h):
        for i in range(2):
            cg1f[h, i].wait_recv()
        to_y(h, 2, h * 8 + yh * 4 + x_at(2))

    def y_done(h):
        for j in range(4):
            cg1y[h, j].wait_recv()

    pair = {}

    def output(h, a):
        rows = slice(8 * h, 8 * h + 8)
        which = (0,) if a == 0 else (1, 2)
        left = {i: (all0[i, rows].reshape(8 * B, CUT), all1[i, rows].reshape(8 * B, G)) for i in which}
        for n in range(2):
            cols = slice(n * 512, n * 512 + 512)
            if a == 0:
                value = dot(left[0][0], dw[:CUT, cols]) + dot(left[0][1], dw[CUT:, cols])
            else:
                value = (dot_t(left[1][0], gw[cols, :CUT]) + dot_t(left[1][1], gw[cols, CUT:])
                         + dot_t(left[2][0], uw[cols, :CUT]) + dot_t(left[2][1], uw[cols, CUT:]))
            value = value.astype(BF).reshape(4, 2, B, 512)
            for core in range(2):
                pk[core, a, 4 * h:4 * h + 4, :, cols] = value[:, core]
        half = pl.ds(4 * h, 4)
        pair[h, a] = remote(pk.at[1 - k, a, half], sk.at[a, half], ks.at[h, a], kr.at[h, a], sibling)

    def outputs(h):
        for a in range(2):
            output(h, a)

    summed = {}

    def add_pair(h, a):
        pair[h, a].wait_recv()
        half = slice(4 * h, 4 * h + 4)
        ps[a, half] = (pk[k, a, half].astype(F32) + sk[a, half].astype(F32)).astype(BF)

    def reduce_first():
        for a in range(2):
            add_pair(0, a)
        summed["far"] = remote(ps.at[:, pl.ds(2, 2)], pz, p4s.at[0], p4r.at[0], plane_peer(2, 0))

    def reduce_first_lo():
        summed["far"].wait_recv()
        pq[...] = (ps[:, 0:2].astype(F32) + pz[...].astype(F32)).astype(BF)
        summed["lo"] = remote(pq.at[:, 1 - yl], py, p4s.at[1], p4r.at[1], lo_peer)

    def reduce_second():
        for a in range(2):
            add_pair(1, a)
            for i, (t, dyl) in enumerate(((2, 0), (3, 0), (2, 1), (3, 1))):
                summed[a, i] = remote(ps.at[a, t * 2 + (yl + dyl) % 2], pr.at[i, a], p4s.at[2 + 4 * a + i],
                                      p4r.at[2 + 4 * a + i], plane_peer(OFFSETS[t], dyl))

    def grads(h, which):
        rows = slice(8 * h, 8 * h + 8)

        def put(acc, out, where, value):
            if h == 0:
                acc[where] = value
            else:
                out[where] = (acc[where] + value).astype(BF)

        for part, lo, width in ((all0, 0, CUT), (all1, CUT, G)):
            cols = slice(lo, lo + width)
            if which < 2:
                right = part[1 + which, rows].reshape(8 * B, width)
                for n in range(4):
                    feats = slice(n * 256, n * 256 + 256)
                    value = dot_rows(buf[0, rows, :, feats].reshape(8 * B, 256), right)
                    put((gate_acc, up_acc)[which], (gate_out, up_out)[which], (feats, cols), value)
            else:
                left = part[0, rows].reshape(8 * B, width)
                for n in range(4):
                    feats = slice(n * 256, n * 256 + 256)
                    value = dot_rows(left, buf[1, rows, :, feats].reshape(8 * B, 256))
                    put(down_acc, down_out, (cols, feats), value)

    def finish():
        summed["lo"].wait_recv()
        for a, out in enumerate((mixed_out, tg_out)):
            total = pq[a, yl].astype(F32) + py[a].astype(F32)
            for i in range(4):
                summed[a, i].wait_recv()
                total = total + pr[i, a].astype(F32)
            out[...] = total

    spread_first()
    for cp in weights:
        cp.wait()
    spread_last(0)
    ready(0, 0)
    x_tokens(0)
    spread_last(1)
    ready(0, 1)
    x_first(0)
    y_first(0)
    spread_second(0)
    spread_second(1)
    x_second(0)
    ready(1, 0)
    x_tokens(1)
    ready(1, 1)
    x_first(1)
    y_first(1)
    y_second(0)
    x_third(0)
    y_third(0)
    x_second(1)
    x_gather(0)
    y_gather(0)
    x_gather_second(0)
    y_second(1)
    x_third(1)
    y_forward(0)
    y_third(1)
    x_gather(1)
    x_forward(0)
    y_gather(1)
    y_forward_last(0)
    x_gather_second(1)
    y_forward(1)
    x_forward(1)
    x_done(0)
    y_done(0)
    outputs(0)
    y_forward_last(1)
    reduce_first()
    grads(0, 0)
    reduce_first_lo()
    x_done(1)
    y_done(1)
    outputs(1)
    reduce_second()
    grads(0, 1)
    grads(0, 2)
    for which in range(3):
        grads(1, which)
    finish()
    for cp in sends:
        cp.wait_send()


def body(tokens, gate_weight, up_weight, down_weight, cotangent):
    dma = lambda *shape: [pltpu.SemaphoreType.DMA(shape)] * 2
    vmem = lambda *shape: pltpu.VMEM(shape, BF)
    whole = pl.BlockSpec(memory_space=pltpu.HBM)
    mixed, token_grad, gate_total, up_total, down_total = pl.pallas_call(
        kernel,
        out_shape=(
            jax.ShapeDtypeStruct((B, D), F32),
            jax.ShapeDtypeStruct((B, D), F32),
            jax.ShapeDtypeStruct((D, F), BF),
            jax.ShapeDtypeStruct((D, F), BF),
            jax.ShapeDtypeStruct((F, D), BF),
        ),
        in_specs=[whole] * 5,
        out_specs=(pl.BlockSpec(memory_space=pltpu.VMEM),) * 5,
        scratch_shapes=[
            vmem(2, 16, B, D), vmem(D, F), vmem(D, F), vmem(F, D),
            vmem(2, 3, 8, B, CUT), vmem(2, 3, 8, B, G),
            vmem(2, 2, 3, B, CUT), vmem(2, 2, 3, B, CUT), vmem(2, 2, 3, B, CUT),
            vmem(2, 3, 2, B, CUT), vmem(2, 3, B, CUT),
            vmem(2, 4, 3, B, G), vmem(2, 4, 3, B, G),
            vmem(2, 3, 3, B, PIECE), vmem(2, 3, 3, B, G - PIECE),
            vmem(3, 16, B, CUT), vmem(3, 16, B, G),
            vmem(2, 2, 8, B, D), vmem(2, 8, B, D), vmem(2, 8, B, D),
            vmem(2, 2, B, D), vmem(2, 2, B, D), vmem(2, B, D), vmem(4, 2, B, D),
            pltpu.VMEM((D, F), F32), pltpu.VMEM((D, F), F32), pltpu.VMEM((F, D), F32),
            pltpu.SemaphoreType.DMA((3,)), pltpu.SemaphoreType.DMA((2,)),
            *dma(2, 7), *dma(2, 8),
            *dma(2, 2), *dma(2, 2), *dma(2, 2), *dma(2), *dma(2, 4), *dma(2, 3), *dma(2, 3),
            *dma(2), *dma(2, 2, 2), *dma(2, 2), *dma(2, 2), *dma(2, 2), *dma(2, 4),
            *dma(2, 2), *dma(10),
        ],
        compiler_params=pltpu.CompilerParams(
            collective_id=0, has_side_effects=True, vmem_limit_bytes=48 * 2**20
        ),
    )(tokens, cotangent, gate_weight, up_weight, down_weight)
    return (mixed, token_grad, gate_total.astype(F32), up_total.astype(F32), down_total.astype(F32))


def solution(mesh):
    placed = (
        P(("depth", "col"), "row"),
        P("row", ("col", "depth")),
        P("row", ("col", "depth")),
        P(("col", "depth"), "row"),
        P(("depth", "col"), "row"),
    )
    return jax.shard_map(
        body,
        mesh=mesh,
        in_specs=placed,
        out_specs=(
            P(("depth", "col"), "row"),
            P(("depth", "col"), "row"),
            P("row", ("col", "depth")),
            P("row", ("col", "depth")),
            P(("col", "depth"), "row"),
        ),
        check_vma=False,
    )
```

```python
import functools

import jax
import jax.numpy as jnp
from jax import lax
from jax.experimental import pallas as pl
from jax.experimental.pallas import tpu as pltpu
from jax.sharding import PartitionSpec as P

MESH = pl.DeviceIdType.MESH
BF = jnp.bfloat16
F32 = jnp.float32
OFFSETS = (0, 2, 1, 3)
B = 48
D = 1024
F = 896
CUT = 512
G = F - CUT
PIECE = 256


def dot(a, b):
    return jnp.dot(a, b, preferred_element_type=F32)


def dot_t(a, b):
    return lax.dot_general(a, b, (((1,), (1,)), ((), ())), preferred_element_type=F32)


def dot_rows(a, b):
    return lax.dot_general(a, b, (((0,), (0,)), ((), ())), preferred_element_type=F32)


def kernel(tok_in, cot_in, gw_in, uw_in, dw_in,
           mixed_out, tg_out, gate_out, up_out, down_out,
           buf, gw, uw, dw, part0, part1, xa, xd, xc, s0, r0y, y1, s1, ya, yb, all0, all1,
           pk, sk, ps, pz, pq, py, pr,
           w_sem, l_sem, p1s, p1r, fs, fr,
           xa_s, xa_r, xd_s, xd_r, xc_s, xc_r, r0y_s, r0y_r, y1_s, y1_r, ya_s, ya_r, yb_s, yb_r,
           g0y_s, g0y_r, g0x_s, g0x_r, g0f_s, g0f_r, g1x_s, g1x_r, g1f_s, g1f_r, g1y_s, g1y_r,
           ks, kr, p4s, p4r):
    row, col, z = lax.axis_index("row"), lax.axis_index("col"), lax.axis_index("depth")
    x, yh = row // 2, row % 2
    yl, k = col // 2, col % 2
    turn = 1 - 2 * k
    mate = (1 - yl) * 2 + k

    sibling = (row, yl * 2 + (1 - k), z)
    y_peer = (x * 2 + (1 - yh), col, z)
    lo_peer = (row, mate, z)

    def x_at(dx):
        return (x + dx + 8) % 4

    def x_peer(dx):
        return (x_at(dx) * 2 + yh, col, z)

    def plane_peer(dz, dyl):
        return (row, ((yl + dyl) % 2) * 2 + k, (z + dz) % 4)

    others = [(t, dyl) for t in range(4) for dyl in range(2) if (t, dyl) != (0, 0)]
    sends = []

    def remote(src, dst, ssem, rsem, dev):
        cp = pltpu.make_async_remote_copy(src_ref=src, dst_ref=dst, send_sem=ssem, recv_sem=rsem,
                                          device_id=dev, device_id_type=MESH)
        cp.start()
        sends.append(cp)
        return cp

    weights = [pltpu.make_async_copy(a, b, w_sem.at[i])
               for i, (a, b) in enumerate(((gw_in, gw), (uw_in, uw), (dw_in, dw)))]
    own = [pltpu.make_async_copy(a, buf.at[i, col], l_sem.at[i]) for i, a in enumerate((tok_in, cot_in))]
    for cp in own + weights:
        cp.start()

    barrier = pltpu.get_barrier_semaphore()
    peers = [sibling, y_peer] + [x_peer(dx) for dx in (1, 3)]
    peers += [plane_peer(OFFSETS[t], dyl) for t, dyl in others]
    for dev in peers:
        pl.semaphore_signal(barrier, inc=1, device_id=dev, device_id_type=MESH)
    pl.semaphore_wait(barrier, len(peers))

    moved, handed = {}, {}

    def share(name, a, i, src, dst, dev):
        moved[name, a] = remote(buf.at[a, src], buf.at[a, dst], p1s.at[a, i], p1r.at[a, i], dev)

    def hand_on(a, i, slot):
        handed[a, i] = remote(buf.at[a, slot], buf.at[a, slot], fs.at[a, i], fr.at[a, i], sibling)

    def spread_first():
        for a in range(2):
            own[a].wait()
            share("lo", a, 0, col, col, lo_peer)
            share("far", a, 1, col, 4 + col, plane_peer(2, 0))
            share("far_lo", a, 6, col, 4 + col, plane_peer(2, 1))
            hand_on(a, 0, col)
        for a in range(2):
            moved["lo", a].wait_recv()
            hand_on(a, 1, mate)
            moved["far", a].wait_recv()
            hand_on(a, 2, 4 + col)
            for i, (t, slot) in enumerate(((2, col), (3, col), (2, mate), (3, mate))):
                share((t, i // 2), a, 2 + i, slot, 4 * t + slot, plane_peer(-OFFSETS[t], 0))

    def spread_last(a):
        moved["far_lo", a].wait_recv()
        hand_on(a, 3, 4 + mate)

    def spread_second(a):
        for i, slot in enumerate((col, mate)):
            for t in (2, 3):
                moved[(t, i), a].wait_recv()
                hand_on(a, 2 * t + i, 4 * t + slot)

    def ready(h, a):
        for i in range(4 * h, 4 * h + 4):
            handed[a, i].wait_recv()

    def tokens_part(h, dst, lo, width):
        rows = buf[0, 8 * h:8 * h + 8].reshape(8 * B, D)
        for i, weight in enumerate((gw, uw)):
            dst[h, i] = dot(rows, weight[:, lo:lo + width]).astype(BF).reshape(8, B, width)

    def cotangent_part(h, dst, lo, width):
        rows = buf[1, 8 * h:8 * h + 8].reshape(8 * B, D)
        dst[h, 2] = dot_t(rows, dw[lo:lo + width, :]).astype(BF).reshape(8, B, width)

    def activate(total, dst, slot):
        gate, up, hidden_grad = total[0], total[1], total[2]
        sigma = jax.nn.sigmoid(gate)
        activated = gate * sigma
        dst[0, slot] = (activated * up).astype(BF)
        dst[1, slot] = (hidden_grad * up * sigma * (1.0 + gate * (1.0 - sigma))).astype(BF)
        dst[2, slot] = (hidden_grad * activated).astype(BF)

    cxa, cxd, cxc, cr0 = {}, {}, {}, {}

    def x_tokens(h):
        tokens_part(h, part0, 0, CUT)

    def x_first(h):
        cotangent_part(h, part0, 0, CUT)
        cxa[h] = [remote(part0.at[h, :, x_at(2) * 2 + i], xa.at[h, i], xa_s.at[h, i], xa_r.at[h, i], x_peer(1 - 2 * i))
                  for i in range(2)]
        cxd[h] = [remote(part0.at[h, :, x_at(1 - 2 * i) * 2 + 1 - i], xd.at[h, i], xd_s.at[h, i], xd_r.at[h, i],
                         x_peer(1 - 2 * i)) for i in range(2)]

    def x_second(h):
        cxc[h] = []
        for i in range(2):
            cxa[h][i].wait_recv()
            xa[h, i] = (xa[h, i].astype(F32) + part0[h, :, x_at(1 - 2 * i) * 2 + i].astype(F32)).astype(BF)
            cxc[h].append(remote(xa.at[h, i], xc.at[h, i], xc_s.at[h, i], xc_r.at[h, i], x_peer(1 - 2 * i)))

    def x_third(h):
        for cp in cxd[h] + cxc[h]:
            cp.wait_recv()
        for i in range(2):
            s0[h, :, i] = (part0[h, :, x * 2 + i].astype(F32) + xd[h, 1 - i].astype(F32)
                           + xc[h, i].astype(F32)).astype(BF)
        cr0[h] = remote(s0.at[h, :, 1 - yh], r0y.at[h], r0y_s.at[h], r0y_r.at[h], y_peer)

    cy1, cya, cyb = {}, {}, {}

    def y_first(h):
        tokens_part(h, part1, CUT, G)
        cotangent_part(h, part1, CUT, G)
        cy1[h] = {j: remote(part1.at[h, :, (1 - yh) * 4 + x_at(turn * j)], y1.at[h, j], y1_s.at[h, j], y1_r.at[h, j],
                            y_peer) for j in (2, 1, 3, 0)}
        cya[h], cyb[h] = {}, {}

    def lap(h, kind, src, ways):
        if "a" in ways:
            cya[h][kind] = remote(src.at[:, :, pl.ds(0, PIECE)], ya.at[h, kind], ya_s.at[h, kind], ya_r.at[h, kind],
                                  x_peer(turn if kind != 1 else -turn))
        if "b" in ways:
            cyb[h][kind] = remote(src.at[:, :, pl.ds(PIECE, G - PIECE)], yb.at[h, kind], yb_s.at[h, kind],
                                  yb_r.at[h, kind], x_peer(-turn if kind != 1 else turn))

    def y_second(h):
        for j in (2, 1, 3, 0):
            cy1[h][j].wait_recv()
            s1[h, j] = (part1[h, :, yh * 4 + x_at(turn * j)].astype(F32) + y1[h, j].astype(F32)).astype(BF)
            if j == 2:
                lap(h, 0, s1.at[h, 2], "ab")
            elif j == 1:
                lap(h, 1, s1.at[h, 1], "b")
            elif j == 3:
                lap(h, 1, s1.at[h, 3], "a")

    def y_third(h):
        cya[h][0].wait_recv()
        s1[h, 1, :, :, :PIECE] = (s1[h, 1, :, :, :PIECE].astype(F32) + ya[h, 0].astype(F32)).astype(BF)
        lap(h, 2, s1.at[h, 1], "a")
        cyb[h][0].wait_recv()
        s1[h, 3, :, :, PIECE:] = (s1[h, 3, :, :, PIECE:].astype(F32) + yb[h, 0].astype(F32)).astype(BF)
        lap(h, 2, s1.at[h, 3], "b")

    cg0y, cg0x, cg0f, cg1x, cg1f, cg1y = {}, {}, {}, {}, {}, {}

    def gather0(h, slot, kind):
        for i in range(2):
            cg0x[h, i, kind] = remote(all0.at[:, slot], all0.at[:, slot], g0x_s.at[h, i, kind], g0x_r.at[h, i, kind],
                                      x_peer(1 - 2 * i))

    def x_gather(h):
        cr0[h].wait_recv()
        slot = h * 8 + x * 2 + yh
        activate(s0[h, :, yh].astype(F32) + r0y[h].astype(F32), all0, slot)
        cg0y[h] = remote(all0.at[:, slot], all0.at[:, slot], g0y_s.at[h], g0y_r.at[h], y_peer)
        gather0(h, slot, 0)

    def x_gather_second(h):
        cg0y[h].wait_recv()
        gather0(h, h * 8 + x * 2 + 1 - yh, 1)

    def x_forward(h):
        for i, slot in enumerate((h * 8 + x_at(-1) * 2 + yh, h * 8 + x_at(1) * 2 + 1 - yh)):
            cg0x[h, i, i].wait_recv()
            cg0f[h, i] = remote(all0.at[:, slot], all0.at[:, slot], g0f_s.at[h, i], g0f_r.at[h, i], x_peer(1 - 2 * i))

    def x_done(h):
        for cp in (cg0x[h, 0, 1], cg0x[h, 1, 0], cg0f[h, 0], cg0f[h, 1]):
            cp.wait_recv()

    def to_y(h, j, slot):
        cg1y[h, j] = remote(all1.at[:, slot], all1.at[:, slot], g1y_s.at[h, j], g1y_r.at[h, j], y_peer)

    def y_gather(h):
        for cp in (cya[h][1], cya[h][2], cyb[h][1], cyb[h][2]):
            cp.wait_recv()
        mine = s1[h, 0].astype(F32)
        left = mine[:, :, :PIECE] + ya[h, 1].astype(F32) + ya[h, 2].astype(F32)
        right = mine[:, :, PIECE:] + yb[h, 1].astype(F32) + yb[h, 2].astype(F32)
        slot = h * 8 + yh * 4 + x
        activate(jnp.concatenate([left, right], axis=2), all1, slot)
        for i in range(2):
            cg1x[h, i] = remote(all1.at[:, slot], all1.at[:, slot], g1x_s.at[h, i], g1x_r.at[h, i],
                                x_peer(turn * (1 - 2 * i)))
        to_y(h, 0, slot)

    def y_forward(h):
        for i, (lo, width) in enumerate(((0, PIECE), (PIECE, G - PIECE))):
            slot = h * 8 + yh * 4 + x_at(turn * (2 * i - 1))
            cg1x[h, i].wait_recv()
            piece = all1.at[:, slot, :, pl.ds(lo, width)]
            cg1f[h, i] = remote(piece, piece, g1f_s.at[h, i], g1f_r.at[h, i], x_peer(turn * (1 - 2 * i)))
            to_y(h, 3 - 2 * i, slot)

    def y_forward_last(h):
        for i in range(2):
            cg1f[h, i].wait_recv()
        to_y(h, 2, h * 8 + yh * 4 + x_at(2))

    def y_done(h):
        for j in range(4):
            cg1y[h, j].wait_recv()

    pair = {}

    def output(h, a):
        rows = slice(8 * h, 8 * h + 8)
        which = (0,) if a == 0 else (1, 2)
        left = {i: (all0[i, rows].reshape(8 * B, CUT), all1[i, rows].reshape(8 * B, G)) for i in which}
        for n in range(2):
            cols = slice(n * 512, n * 512 + 512)
            if a == 0:
                value = dot(left[0][0], dw[:CUT, cols]) + dot(left[0][1], dw[CUT:, cols])
            else:
                value = (dot_t(left[1][0], gw[cols, :CUT]) + dot_t(left[1][1], gw[cols, CUT:])
                         + dot_t(left[2][0], uw[cols, :CUT]) + dot_t(left[2][1], uw[cols, CUT:]))
            value = value.astype(BF).reshape(4, 2, B, 512)
            for core in range(2):
                pk[core, a, 4 * h:4 * h + 4, :, cols] = value[:, core]
        half = pl.ds(4 * h, 4)
        pair[h, a] = remote(pk.at[1 - k, a, half], sk.at[a, half], ks.at[h, a], kr.at[h, a], sibling)

    summed = {}

    def add_pair(h, a):
        pair[h, a].wait_recv()
        half = slice(4 * h, 4 * h + 4)
        ps[a, half] = (pk[k, a, half].astype(F32) + sk[a, half].astype(F32)).astype(BF)

    def reduce_first():
        for a in range(2):
            add_pair(0, a)
        summed["far"] = remote(ps.at[:, pl.ds(2, 2)], pz, p4s.at[0], p4r.at[0], plane_peer(2, 0))

    def reduce_first_lo():
        summed["far"].wait_recv()
        pq[...] = (ps[:, 0:2].astype(F32) + pz[...].astype(F32)).astype(BF)
        summed["lo"] = remote(pq.at[:, 1 - yl], py, p4s.at[1], p4r.at[1], lo_peer)

    def reduce_second(a):
        add_pair(1, a)
        for i, (t, dyl) in enumerate(((2, 0), (3, 0), (2, 1), (3, 1))):
            summed[a, i] = remote(ps.at[a, t * 2 + (yl + dyl) % 2], pr.at[i, a], p4s.at[2 + 4 * a + i],
                                  p4r.at[2 + 4 * a + i], plane_peer(OFFSETS[t], dyl))

    def grads(h, which):
        rows = slice(8 * h, 8 * h + 8)
        out = (gate_out, up_out, down_out)[which]

        def put(where, value):
            out[where] = value if h == 0 else out[where] + value

        for part, lo, width in ((all0, 0, CUT), (all1, CUT, G)):
            cols = slice(lo, lo + width)
            if which < 2:
                right = part[1 + which, rows].reshape(8 * B, width)
                for n in range(4):
                    feats = slice(n * 256, n * 256 + 256)
                    put((feats, cols), dot_rows(buf[0, rows, :, feats].reshape(8 * B, 256), right))
            else:
                left = part[0, rows].reshape(8 * B, width)
                for n in range(4):
                    feats = slice(n * 256, n * 256 + 256)
                    put((cols, feats), dot_rows(left, buf[1, rows, :, feats].reshape(8 * B, 256)))

    def finish():
        summed["lo"].wait_recv()
        for a, out in enumerate((mixed_out, tg_out)):
            total = pq[a, yl].astype(F32) + py[a].astype(F32)
            for i in range(4):
                summed[a, i].wait_recv()
                total = total + pr[i, a].astype(F32)
            out[...] = total

    spread_first()
    for cp in weights:
        cp.wait()
    spread_last(0)
    spread_last(1)
    ready(0, 0)
    x_tokens(0)
    ready(0, 1)
    x_first(0)
    y_first(0)
    spread_second(0)
    spread_second(1)
    ready(1, 0)
    x_tokens(1)
    ready(1, 1)
    x_first(1)
    x_second(0)
    y_first(1)
    y_second(0)
    y_third(0)
    x_third(0)
    x_second(1)
    y_gather(0)
    y_second(1)
    x_gather(0)
    y_third(1)
    x_gather_second(0)
    x_third(1)
    y_forward(0)
    x_forward(0)
    y_forward_last(0)
    x_gather(1)
    x_done(0)
    y_gather(1)
    y_done(0)
    output(0, 0)
    output(0, 1)
    reduce_first()
    x_gather_second(1)
    grads(0, 1)
    y_forward(1)
    grads(0, 0)
    grads(0, 2)
    x_forward(1)
    y_forward_last(1)
    reduce_first_lo()
    y_done(1)
    x_done(1)
    output(1, 0)
    reduce_second(0)
    output(1, 1)
    reduce_second(1)
    grads(1, 2)
    grads(1, 0)
    grads(1, 1)
    finish()
    for cp in sends:
        cp.wait_send()


def write(*refs):
    sems = refs[10]
    copies = [pltpu.make_async_copy(refs[i], refs[5 + i], sems.at[i]) for i in (2, 3, 4, 0, 1)]
    for cp in copies:
        cp.start()
    for cp in copies:
        cp.wait()


def body(tokens, gate_weight, up_weight, down_weight, cotangent):
    dma = lambda *shape: [pltpu.SemaphoreType.DMA(shape)] * 2
    vmem = lambda *shape: pltpu.VMEM(shape, BF)
    whole = pl.BlockSpec(memory_space=pltpu.HBM)
    results = pl.pallas_call(
        kernel,
        out_shape=(
            jax.ShapeDtypeStruct((B, D), F32),
            jax.ShapeDtypeStruct((B, D), F32),
            jax.ShapeDtypeStruct((D, F), F32),
            jax.ShapeDtypeStruct((D, F), F32),
            jax.ShapeDtypeStruct((F, D), F32),
        ),
        in_specs=[whole] * 5,
        out_specs=(pl.BlockSpec(memory_space=pltpu.VMEM),) * 5,
        scratch_shapes=[
            vmem(2, 16, B, D), vmem(D, F), vmem(D, F), vmem(F, D),
            vmem(2, 3, 8, B, CUT), vmem(2, 3, 8, B, G),
            vmem(2, 2, 3, B, CUT), vmem(2, 2, 3, B, CUT), vmem(2, 2, 3, B, CUT),
            vmem(2, 3, 2, B, CUT), vmem(2, 3, B, CUT),
            vmem(2, 4, 3, B, G), vmem(2, 4, 3, B, G),
            vmem(2, 3, 3, B, PIECE), vmem(2, 3, 3, B, G - PIECE),
            vmem(3, 16, B, CUT), vmem(3, 16, B, G),
            vmem(2, 2, 8, B, D), vmem(2, 8, B, D), vmem(2, 8, B, D),
            vmem(2, 2, B, D), vmem(2, 2, B, D), vmem(2, B, D), vmem(4, 2, B, D),
            pltpu.SemaphoreType.DMA((3,)), pltpu.SemaphoreType.DMA((2,)),
            *dma(2, 7), *dma(2, 8),
            *dma(2, 2), *dma(2, 2), *dma(2, 2), *dma(2), *dma(2, 4), *dma(2, 3), *dma(2, 3),
            *dma(2), *dma(2, 2, 2), *dma(2, 2), *dma(2, 2), *dma(2, 2), *dma(2, 4),
            *dma(2, 2), *dma(10),
        ],
        compiler_params=pltpu.CompilerParams(
            collective_id=0, has_side_effects=True, vmem_limit_bytes=38 * 2**20
        ),
    )(*(pltpu.with_memory_space_constraint(a, pltpu.HBM)
        for a in (tokens, cotangent, gate_weight, up_weight, down_weight)))
    return pl.pallas_call(
        write,
        out_shape=tuple(jax.ShapeDtypeStruct(r.shape, F32) for r in results),
        in_specs=[pl.BlockSpec(memory_space=pltpu.VMEM)] * 5,
        out_specs=(pl.BlockSpec(memory_space=pl.ANY),) * 5,
        scratch_shapes=[pltpu.SemaphoreType.DMA((5,))],
        compiler_params=pltpu.CompilerParams(vmem_limit_bytes=2**20),
    )(*(pltpu.with_memory_space_constraint(r, pltpu.VMEM) for r in results))


def solution(mesh):
    placed = (
        P(("depth", "col"), "row"),
        P("row", ("col", "depth")),
        P("row", ("col", "depth")),
        P(("col", "depth"), "row"),
        P(("depth", "col"), "row"),
    )
    return jax.shard_map(
        body,
        mesh=mesh,
        in_specs=placed,
        out_specs=(
            P(("depth", "col"), "row"),
            P(("depth", "col"), "row"),
            P("row", ("col", "depth")),
            P("row", ("col", "depth")),
            P(("col", "depth"), "row"),
        ),
        check_vma=False,
    )
```

```python
import functools

import jax
import jax.numpy as jnp
from jax import lax
from jax.experimental import pallas as pl
from jax.experimental.pallas import tpu as pltpu
from jax.sharding import PartitionSpec as P

MESH = pl.DeviceIdType.MESH
BF = jnp.bfloat16
F32 = jnp.float32
OFFSETS = (0, 2, 1, 3)
B = 48
D = 1024
F = 896
CUT = 512
G = F - CUT
PIECE = 256


def dot(a, b):
    return jnp.dot(a, b, preferred_element_type=F32)


def dot_t(a, b):
    return lax.dot_general(a, b, (((1,), (1,)), ((), ())), preferred_element_type=F32)


def dot_rows(a, b):
    return lax.dot_general(a, b, (((0,), (0,)), ((), ())), preferred_element_type=F32)


def kernel(tok_in, cot_in, gw_in, uw_in, dw_in,
           mixed_out, tg_out, gate_out, up_out, down_out,
           buf, gw, uw, dw, part0, part1, xa, xd, xc, s0, r0y, y1, s1, ya, yb, all0, all1,
           pk, sk, ps, pz, pq, py, pr,
           w_sem, l_sem, p1s, p1r, fs, fr,
           xa_s, xa_r, xd_s, xd_r, xc_s, xc_r, r0y_s, r0y_r, y1_s, y1_r, ya_s, ya_r, yb_s, yb_r,
           g0y_s, g0y_r, g0x_s, g0x_r, g0f_s, g0f_r, g1x_s, g1x_r, g1f_s, g1f_r, g1y_s, g1y_r,
           ks, kr, p4s, p4r):
    row, col, z = lax.axis_index("row"), lax.axis_index("col"), lax.axis_index("depth")
    x, yh = row // 2, row % 2
    yl, k = col // 2, col % 2
    turn = 1 - 2 * k
    mate = (1 - yl) * 2 + k

    sibling = (row, yl * 2 + (1 - k), z)
    y_peer = (x * 2 + (1 - yh), col, z)
    lo_peer = (row, mate, z)

    def x_at(dx):
        return (x + dx + 8) % 4

    def x_peer(dx):
        return (x_at(dx) * 2 + yh, col, z)

    def plane_peer(dz, dyl):
        return (row, ((yl + dyl) % 2) * 2 + k, (z + dz) % 4)

    others = [(t, dyl) for t in range(4) for dyl in range(2) if (t, dyl) != (0, 0)]
    sends = []

    def remote(src, dst, ssem, rsem, dev):
        cp = pltpu.make_async_remote_copy(src_ref=src, dst_ref=dst, send_sem=ssem, recv_sem=rsem,
                                          device_id=dev, device_id_type=MESH)
        cp.start()
        sends.append(cp)
        return cp

    weights = [pltpu.make_async_copy(a, b, w_sem.at[i])
               for i, (a, b) in enumerate(((gw_in, gw), (uw_in, uw), (dw_in, dw)))]
    own = [pltpu.make_async_copy(a, buf.at[i, col], l_sem.at[i]) for i, a in enumerate((tok_in, cot_in))]
    for cp in own + weights:
        cp.start()

    barrier = pltpu.get_barrier_semaphore()
    peers = [sibling, y_peer] + [x_peer(dx) for dx in (1, 3)]
    peers += [plane_peer(OFFSETS[t], dyl) for t, dyl in others]
    for dev in peers:
        pl.semaphore_signal(barrier, inc=1, device_id=dev, device_id_type=MESH)
    pl.semaphore_wait(barrier, len(peers))

    moved, handed = {}, {}

    def share(name, a, i, src, dst, dev):
        moved[name, a] = remote(buf.at[a, src], buf.at[a, dst], p1s.at[a, i], p1r.at[a, i], dev)

    def hand_on(a, i, slot):
        handed[a, i] = remote(buf.at[a, slot], buf.at[a, slot], fs.at[a, i], fr.at[a, i], sibling)

    def spread_first():
        for a in range(2):
            own[a].wait()
            share("lo", a, 0, col, col, lo_peer)
            share("far", a, 1, col, 4 + col, plane_peer(2, 0))
            hand_on(a, 0, col)
        for a in range(2):
            moved["lo", a].wait_recv()
            hand_on(a, 1, mate)
            moved["far", a].wait_recv()
            share("far_lo", a, 6, 4 + col, 4 + col, lo_peer)
            hand_on(a, 2, 4 + col)
            for i, (t, slot) in enumerate(((2, col), (3, col), (2, mate), (3, mate))):
                share((t, i // 2), a, 2 + i, slot, 4 * t + slot, plane_peer(-OFFSETS[t], 0))

    def spread_last(a):
        moved["far_lo", a].wait_recv()
        hand_on(a, 3, 4 + mate)

    def spread_second(a):
        for i, slot in enumerate((col, mate)):
            for t in (2, 3):
                moved[(t, i), a].wait_recv()
                hand_on(a, 2 * t + i, 4 * t + slot)

    def ready(h, a):
        for i in range(4 * h, 4 * h + 4):
            handed[a, i].wait_recv()

    def tokens_part(h, dst, lo, width):
        rows = buf[0, 8 * h:8 * h + 8].reshape(8 * B, D)
        for i, weight in enumerate((gw, uw)):
            dst[h, i] = dot(rows, weight[:, lo:lo + width]).astype(BF).reshape(8, B, width)

    def cotangent_part(h, dst, lo, width):
        rows = buf[1, 8 * h:8 * h + 8].reshape(8 * B, D)
        dst[h, 2] = dot_t(rows, dw[lo:lo + width, :]).astype(BF).reshape(8, B, width)

    def activate(total, dst, slot):
        gate, up, hidden_grad = total[0], total[1], total[2]
        sigma = jax.nn.sigmoid(gate)
        activated = gate * sigma
        dst[0, slot] = (activated * up).astype(BF)
        dst[1, slot] = (hidden_grad * up * sigma * (1.0 + gate * (1.0 - sigma))).astype(BF)
        dst[2, slot] = (hidden_grad * activated).astype(BF)

    cxa, cxd, cxc, cr0 = {}, {}, {}, {}

    def x_tokens(h):
        tokens_part(h, part0, 0, CUT)

    def x_alpha(h):
        cotangent_part(h, part0, 0, CUT)
        cxa[h] = [remote(part0.at[h, :, x_at(2) * 2 + i], xa.at[h, i], xa_s.at[h, i], xa_r.at[h, i], x_peer(1 - 2 * i))
                  for i in range(2)]

    def x_direct(h):
        cxd[h] = [remote(part0.at[h, :, x_at(1 - 2 * i) * 2 + 1 - i], xd.at[h, i], xd_s.at[h, i], xd_r.at[h, i],
                         x_peer(1 - 2 * i)) for i in range(2)]

    def x_second(h, i):
        cxa[h][i].wait_recv()
        xa[h, i] = (xa[h, i].astype(F32) + part0[h, :, x_at(1 - 2 * i) * 2 + i].astype(F32)).astype(BF)
        cxc[h, i] = remote(xa.at[h, i], xc.at[h, i], xc_s.at[h, i], xc_r.at[h, i], x_peer(1 - 2 * i))

    def x_third(h):
        for cp in cxd[h] + [cxc[h, 0], cxc[h, 1]]:
            cp.wait_recv()
        for i in range(2):
            s0[h, :, i] = (part0[h, :, x * 2 + i].astype(F32) + xd[h, 1 - i].astype(F32)
                           + xc[h, i].astype(F32)).astype(BF)
        cr0[h] = remote(s0.at[h, :, 1 - yh], r0y.at[h], r0y_s.at[h], r0y_r.at[h], y_peer)

    cy1, cya, cyb = {}, {}, {}

    def y_partial(h):
        tokens_part(h, part1, CUT, G)
        cotangent_part(h, part1, CUT, G)
        cya[h], cyb[h] = {}, {}

    def y_send(h, j):
        cy1[h, j] = remote(part1.at[h, :, (1 - yh) * 4 + x_at(turn * j)], y1.at[h, j], y1_s.at[h, j], y1_r.at[h, j],
                           y_peer)

    def lap(h, kind, src, ways):
        if "a" in ways:
            cya[h][kind] = remote(src.at[:, :, pl.ds(0, PIECE)], ya.at[h, kind], ya_s.at[h, kind], ya_r.at[h, kind],
                                  x_peer(turn if kind != 1 else -turn))
        if "b" in ways:
            cyb[h][kind] = remote(src.at[:, :, pl.ds(PIECE, G - PIECE)], yb.at[h, kind], yb_s.at[h, kind],
                                  yb_r.at[h, kind], x_peer(-turn if kind != 1 else turn))

    def y_sum(h, j):
        cy1[h, j].wait_recv()
        s1[h, j] = (part1[h, :, yh * 4 + x_at(turn * j)].astype(F32) + y1[h, j].astype(F32)).astype(BF)
        if j:
            lap(h, j % 2, s1.at[h, j], ("b", "ab", "a")[j - 1])

    def y_third(h, i):
        if i == 0:
            cya[h][0].wait_recv()
            s1[h, 1, :, :, :PIECE] = (s1[h, 1, :, :, :PIECE].astype(F32) + ya[h, 0].astype(F32)).astype(BF)
            lap(h, 2, s1.at[h, 1], "a")
        else:
            cyb[h][0].wait_recv()
            s1[h, 3, :, :, PIECE:] = (s1[h, 3, :, :, PIECE:].astype(F32) + yb[h, 0].astype(F32)).astype(BF)
            lap(h, 2, s1.at[h, 3], "b")

    cg0y, cg0x, cg0f, cg1x, cg1f, cg1y = {}, {}, {}, {}, {}, {}

    def gather0(h, slot, kind):
        for i in range(2):
            cg0x[h, i, kind] = remote(all0.at[:, slot], all0.at[:, slot], g0x_s.at[h, i, kind], g0x_r.at[h, i, kind],
                                      x_peer(1 - 2 * i))

    def x_gather(h):
        cr0[h].wait_recv()
        slot = h * 8 + x * 2 + yh
        activate(s0[h, :, yh].astype(F32) + r0y[h].astype(F32), all0, slot)
        cg0y[h] = remote(all0.at[:, slot], all0.at[:, slot], g0y_s.at[h], g0y_r.at[h], y_peer)
        gather0(h, slot, 0)

    def x_gather_second(h):
        cg0y[h].wait_recv()
        gather0(h, h * 8 + x * 2 + 1 - yh, 1)

    def x_forward(h, i):
        slot = h * 8 + (x_at(-1) * 2 + yh if i == 0 else x_at(1) * 2 + 1 - yh)
        cg0x[h, i, i].wait_recv()
        cg0f[h, i] = remote(all0.at[:, slot], all0.at[:, slot], g0f_s.at[h, i], g0f_r.at[h, i], x_peer(1 - 2 * i))

    def x_done(h):
        for cp in (cg0x[h, 0, 1], cg0x[h, 1, 0], cg0f[h, 0], cg0f[h, 1]):
            cp.wait_recv()

    def to_y(h, j, slot):
        cg1y[h, j] = remote(all1.at[:, slot], all1.at[:, slot], g1y_s.at[h, j], g1y_r.at[h, j], y_peer)

    def y_gather(h):
        for cp in (cya[h][1], cya[h][2], cyb[h][1], cyb[h][2]):
            cp.wait_recv()
        mine = s1[h, 0].astype(F32)
        left = mine[:, :, :PIECE] + ya[h, 1].astype(F32) + ya[h, 2].astype(F32)
        right = mine[:, :, PIECE:] + yb[h, 1].astype(F32) + yb[h, 2].astype(F32)
        slot = h * 8 + yh * 4 + x
        activate(jnp.concatenate([left, right], axis=2), all1, slot)
        for i in range(2):
            cg1x[h, i] = remote(all1.at[:, slot], all1.at[:, slot], g1x_s.at[h, i], g1x_r.at[h, i],
                                x_peer(turn * (1 - 2 * i)))
        to_y(h, 0, slot)

    def y_forward(h, i):
        lo, width = ((0, PIECE), (PIECE, G - PIECE))[i]
        slot = h * 8 + yh * 4 + x_at(turn * (2 * i - 1))
        cg1x[h, i].wait_recv()
        piece = all1.at[:, slot, :, pl.ds(lo, width)]
        cg1f[h, i] = remote(piece, piece, g1f_s.at[h, i], g1f_r.at[h, i], x_peer(turn * (1 - 2 * i)))
        to_y(h, 3 - 2 * i, slot)

    def y_forward_last(h):
        for i in range(2):
            cg1f[h, i].wait_recv()
        to_y(h, 2, h * 8 + yh * 4 + x_at(2))

    def y_done(h):
        for j in range(4):
            cg1y[h, j].wait_recv()

    pair = {}

    def output(h, a):
        rows = slice(8 * h, 8 * h + 8)
        which = (0,) if a == 0 else (1, 2)
        left = {i: (all0[i, rows].reshape(8 * B, CUT), all1[i, rows].reshape(8 * B, G)) for i in which}
        for n in range(2):
            cols = slice(n * 512, n * 512 + 512)
            if a == 0:
                value = dot(left[0][0], dw[:CUT, cols]) + dot(left[0][1], dw[CUT:, cols])
            else:
                value = (dot_t(left[1][0], gw[cols, :CUT]) + dot_t(left[1][1], gw[cols, CUT:])
                         + dot_t(left[2][0], uw[cols, :CUT]) + dot_t(left[2][1], uw[cols, CUT:]))
            value = value.astype(BF).reshape(4, 2, B, 512)
            for core in range(2):
                pk[core, a, 4 * h:4 * h + 4, :, cols] = value[:, core]
        half = pl.ds(4 * h, 4)
        pair[h, a] = remote(pk.at[1 - k, a, half], sk.at[a, half], ks.at[h, a], kr.at[h, a], sibling)

    summed = {}

    def add_pair(h, a):
        pair[h, a].wait_recv()
        half = slice(4 * h, 4 * h + 4)
        ps[a, half] = (pk[k, a, half].astype(F32) + sk[a, half].astype(F32)).astype(BF)

    def reduce_first():
        for a in range(2):
            add_pair(0, a)
        summed["far"] = remote(ps.at[:, pl.ds(2, 2)], pz, p4s.at[0], p4r.at[0], plane_peer(2, 0))

    def reduce_first_lo():
        summed["far"].wait_recv()
        pq[...] = (ps[:, 0:2].astype(F32) + pz[...].astype(F32)).astype(BF)
        summed["lo"] = remote(pq.at[:, 1 - yl], py, p4s.at[1], p4r.at[1], lo_peer)

    def reduce_second(a):
        add_pair(1, a)
        for i, (t, dyl) in enumerate(((2, 0), (3, 0), (2, 1), (3, 1))):
            summed[a, i] = remote(ps.at[a, t * 2 + (yl + dyl) % 2], pr.at[i, a], p4s.at[2 + 4 * a + i],
                                  p4r.at[2 + 4 * a + i], plane_peer(OFFSETS[t], dyl))

    def grads(h, which):
        rows = slice(8 * h, 8 * h + 8)
        out = (gate_out, up_out, down_out)[which]

        def put(where, value):
            out[where] = value if h == 0 else out[where] + value

        for part, lo, width in ((all0, 0, CUT), (all1, CUT, G)):
            cols = slice(lo, lo + width)
            if which < 2:
                right = part[1 + which, rows].reshape(8 * B, width)
                for n in range(4):
                    feats = slice(n * 256, n * 256 + 256)
                    put((feats, cols), dot_rows(buf[0, rows, :, feats].reshape(8 * B, 256), right))
            else:
                left = part[0, rows].reshape(8 * B, width)
                for n in range(4):
                    feats = slice(n * 256, n * 256 + 256)
                    put((cols, feats), dot_rows(left, buf[1, rows, :, feats].reshape(8 * B, 256)))

    def finish():
        summed["lo"].wait_recv()
        for a, out in enumerate((mixed_out, tg_out)):
            total = pq[a, yl].astype(F32) + py[a].astype(F32)
            for i in range(4):
                summed[a, i].wait_recv()
                total = total + pr[i, a].astype(F32)
            out[...] = total

    spread_first()
    for cp in weights:
        cp.wait()
    spread_last(0)
    spread_last(1)
    ready(0, 0)
    x_tokens(0)
    ready(0, 1)
    y_partial(0)
    y_send(0, 0)
    x_alpha(0)
    spread_second(0)
    ready(1, 0)
    spread_second(1)
    y_send(0, 3)
    y_send(0, 1)
    ready(1, 1)
    y_send(0, 2)
    x_direct(0)
    x_second(0, 0)
    x_second(0, 1)
    x_tokens(1)
    y_partial(1)
    y_send(1, 1)
    x_alpha(1)
    y_sum(0, 1)
    y_sum(0, 2)
    x_direct(1)
    y_send(1, 0)
    x_third(0)
    y_sum(0, 3)
    y_third(0, 1)
    x_second(1, 0)
    y_sum(1, 1)
    x_second(1, 1)
    y_send(1, 2)
    y_third(0, 0)
    y_sum(0, 0)
    y_send(1, 3)
    x_gather(0)
    y_gather(0)
    x_gather_second(0)
    y_sum(1, 2)
    x_third(1)
    y_forward(0, 0)
    y_sum(1, 0)
    y_forward(0, 1)
    y_sum(1, 3)
    y_third(1, 0)
    y_third(1, 1)
    x_forward(0, 1)
    x_forward(0, 0)
    y_forward_last(0)
    y_gather(1)
    x_gather(1)
    x_done(0)
    y_done(0)
    output(0, 0)
    output(0, 1)
    reduce_first()
    y_forward(1, 0)
    y_forward(1, 1)
    x_gather_second(1)
    grads(0, 1)
    y_forward_last(1)
    x_forward(1, 0)
    x_forward(1, 1)
    reduce_first_lo()
    y_done(1)
    x_done(1)
    output(1, 0)
    reduce_second(0)
    output(1, 1)
    grads(0, 2)
    reduce_second(1)
    grads(0, 0)
    grads(1, 0)
    grads(1, 2)
    grads(1, 1)
    finish()
    for cp in sends:
        cp.wait_send()


def write(*refs):
    sems = refs[10]
    copies = [pltpu.make_async_copy(refs[i], refs[5 + i], sems.at[i]) for i in (2, 3, 4, 0, 1)]
    for cp in copies:
        cp.start()
    for cp in copies:
        cp.wait()


def body(tokens, gate_weight, up_weight, down_weight, cotangent):
    dma = lambda *shape: [pltpu.SemaphoreType.DMA(shape)] * 2
    vmem = lambda *shape: pltpu.VMEM(shape, BF)
    whole = pl.BlockSpec(memory_space=pltpu.HBM)
    results = pl.pallas_call(
        kernel,
        out_shape=(
            jax.ShapeDtypeStruct((B, D), F32),
            jax.ShapeDtypeStruct((B, D), F32),
            jax.ShapeDtypeStruct((D, F), F32),
            jax.ShapeDtypeStruct((D, F), F32),
            jax.ShapeDtypeStruct((F, D), F32),
        ),
        in_specs=[whole] * 5,
        out_specs=(pl.BlockSpec(memory_space=pltpu.VMEM),) * 5,
        scratch_shapes=[
            vmem(2, 16, B, D), vmem(D, F), vmem(D, F), vmem(F, D),
            vmem(2, 3, 8, B, CUT), vmem(2, 3, 8, B, G),
            vmem(2, 2, 3, B, CUT), vmem(2, 2, 3, B, CUT), vmem(2, 2, 3, B, CUT),
            vmem(2, 3, 2, B, CUT), vmem(2, 3, B, CUT),
            vmem(2, 4, 3, B, G), vmem(2, 4, 3, B, G),
            vmem(2, 3, 3, B, PIECE), vmem(2, 3, 3, B, G - PIECE),
            vmem(3, 16, B, CUT), vmem(3, 16, B, G),
            vmem(2, 2, 8, B, D), vmem(2, 8, B, D), vmem(2, 8, B, D),
            vmem(2, 2, B, D), vmem(2, 2, B, D), vmem(2, B, D), vmem(4, 2, B, D),
            pltpu.SemaphoreType.DMA((3,)), pltpu.SemaphoreType.DMA((2,)),
            *dma(2, 7), *dma(2, 8),
            *dma(2, 2), *dma(2, 2), *dma(2, 2), *dma(2), *dma(2, 4), *dma(2, 3), *dma(2, 3),
            *dma(2), *dma(2, 2, 2), *dma(2, 2), *dma(2, 2), *dma(2, 2), *dma(2, 4),
            *dma(2, 2), *dma(10),
        ],
        compiler_params=pltpu.CompilerParams(
            collective_id=0, has_side_effects=True, vmem_limit_bytes=38 * 2**20
        ),
    )(*(pltpu.with_memory_space_constraint(a, pltpu.HBM)
        for a in (tokens, cotangent, gate_weight, up_weight, down_weight)))
    return pl.pallas_call(
        write,
        out_shape=tuple(jax.ShapeDtypeStruct(r.shape, F32) for r in results),
        in_specs=[pl.BlockSpec(memory_space=pltpu.VMEM)] * 5,
        out_specs=(pl.BlockSpec(memory_space=pl.ANY),) * 5,
        scratch_shapes=[pltpu.SemaphoreType.DMA((5,))],
        compiler_params=pltpu.CompilerParams(vmem_limit_bytes=2**20),
    )(*(pltpu.with_memory_space_constraint(r, pltpu.VMEM) for r in results))


def solution(mesh):
    placed = (
        P(("depth", "col"), "row"),
        P("row", ("col", "depth")),
        P("row", ("col", "depth")),
        P(("col", "depth"), "row"),
        P(("depth", "col"), "row"),
    )
    return jax.shard_map(
        body,
        mesh=mesh,
        in_specs=placed,
        out_specs=(
            P(("depth", "col"), "row"),
            P(("depth", "col"), "row"),
            P("row", ("col", "depth")),
            P("row", ("col", "depth")),
            P(("col", "depth"), "row"),
        ),
        check_vma=False,
    )
```

```python
import functools

import jax
import jax.numpy as jnp
from jax import lax
from jax.experimental import pallas as pl
from jax.experimental.pallas import tpu as pltpu
from jax.sharding import PartitionSpec as P

MESH = pl.DeviceIdType.MESH
BF = jnp.bfloat16
F32 = jnp.float32
OFFSETS = (0, 2, 1, 3)
B = 48
D = 1024
F = 896
CUT = 512
G = F - CUT
PARTS = 4
PIECE = 256


def dot(a, b):
    return jnp.dot(a, b, preferred_element_type=F32)


def dot_t(a, b):
    return lax.dot_general(a, b, (((1,), (1,)), ((), ())), preferred_element_type=F32)


def dot_rows(a, b):
    return lax.dot_general(a, b, (((0,), (0,)), ((), ())), preferred_element_type=F32)


def kernel(tok_in, cot_in, gw_in, uw_in, dw_in,
           mixed_out, tg_out, gate_out, up_out, down_out,
           buf, gw, uw, dw, part0, part1, xa, xd, xc, s0, r0y, y1, s1, ya, yb, all0, all1,
           pk, sk, ps, pz, pq, py, pr,
           w_sem, l_sem, p1s, p1r, fs, fr,
           xa_s, xa_r, xd_s, xd_r, xc_s, xc_r, r0y_s, r0y_r, y1_s, y1_r, ya_s, ya_r, yb_s, yb_r,
           g0y_s, g0y_r, g0x_s, g0x_r, g0f_s, g0f_r, g1x_s, g1x_r, g1f_s, g1f_r, g1y_s, g1y_r,
           ks, kr, p4s, p4r):
    row, col, z = lax.axis_index("row"), lax.axis_index("col"), lax.axis_index("depth")
    x, yh = row // 2, row % 2
    yl, k = col // 2, col % 2
    turn = 1 - 2 * k
    mate = (1 - yl) * 2 + k

    sibling = (row, yl * 2 + (1 - k), z)
    y_peer = (x * 2 + (1 - yh), col, z)
    lo_peer = (row, mate, z)

    def x_at(dx):
        return (x + dx + 8) % 4

    def x_peer(dx):
        return (x_at(dx) * 2 + yh, col, z)

    def plane_peer(dz, dyl):
        return (row, ((yl + dyl) % 2) * 2 + k, (z + dz) % 4)

    others = [(t, dyl) for t in range(4) for dyl in range(2) if (t, dyl) != (0, 0)]
    sends = []

    def remote(src, dst, ssem, rsem, dev):
        cp = pltpu.make_async_remote_copy(src_ref=src, dst_ref=dst, send_sem=ssem, recv_sem=rsem,
                                          device_id=dev, device_id_type=MESH)
        cp.start()
        sends.append(cp)
        return cp

    weights = [pltpu.make_async_copy(a, b, w_sem.at[i])
               for i, (a, b) in enumerate(((gw_in, gw), (uw_in, uw), (dw_in, dw)))]
    own = [pltpu.make_async_copy(a, buf.at[i, col], l_sem.at[i]) for i, a in enumerate((tok_in, cot_in))]
    for cp in own + weights:
        cp.start()

    barrier = pltpu.get_barrier_semaphore()
    peers = [sibling, y_peer] + [x_peer(dx) for dx in (1, 3)]
    peers += [plane_peer(OFFSETS[t], dyl) for t, dyl in others]
    for dev in peers:
        pl.semaphore_signal(barrier, inc=1, device_id=dev, device_id_type=MESH)
    pl.semaphore_wait(barrier, len(peers))

    moved, handed = {}, {}

    def share(name, a, i, src, dst, dev):
        moved[name, a] = remote(buf.at[a, src], buf.at[a, dst], p1s.at[a, i], p1r.at[a, i], dev)

    def hand_on(a, i, slot):
        handed[a, i] = remote(buf.at[a, slot], buf.at[a, slot], fs.at[a, i], fr.at[a, i], sibling)

    def spread_first():
        for a in range(2):
            own[a].wait()
            share("lo", a, 0, col, col, lo_peer)
            share("far", a, 1, col, 4 + col, plane_peer(2, 0))
            hand_on(a, 0, col)
        for a in range(2):
            moved["lo", a].wait_recv()
            hand_on(a, 1, mate)
            moved["far", a].wait_recv()
            share("far_lo", a, 6, 4 + col, 4 + col, lo_peer)
            hand_on(a, 2, 4 + col)
            for i, (t, slot) in enumerate(((2, col), (3, col), (2, mate), (3, mate))):
                share((t, i // 2), a, 2 + i, slot, 4 * t + slot, plane_peer(-OFFSETS[t], 0))

    def spread_last(a):
        moved["far_lo", a].wait_recv()
        hand_on(a, 3, 4 + mate)

    def spread_second(a):
        for i, slot in enumerate((col, mate)):
            for t in (2, 3):
                moved[(t, i), a].wait_recv()
                hand_on(a, 2 * t + i, 4 * t + slot)

    def ready(h, a):
        for i in range(4 * h, 4 * h + 4):
            handed[a, i].wait_recv()

    def tokens_part(h, dst, lo, width):
        rows = buf[0, 8 * h:8 * h + 8].reshape(8 * B, D)
        for i, weight in enumerate((gw, uw)):
            dst[h, i] = dot(rows, weight[:, lo:lo + width]).astype(BF).reshape(8, B, width)

    def cotangent_part(h, dst, lo, width):
        rows = buf[1, 8 * h:8 * h + 8].reshape(8 * B, D)
        dst[h, 2] = dot_t(rows, dw[lo:lo + width, :]).astype(BF).reshape(8, B, width)

    def activate(total, dst, slot):
        gate, up, hidden_grad = total[0], total[1], total[2]
        sigma = jax.nn.sigmoid(gate)
        activated = gate * sigma
        dst[0, slot] = (activated * up).astype(BF)
        dst[1, slot] = (hidden_grad * up * sigma * (1.0 + gate * (1.0 - sigma))).astype(BF)
        dst[2, slot] = (hidden_grad * activated).astype(BF)

    cxa, cxd, cxc, cr0 = {}, {}, {}, {}

    def x_tokens(h):
        tokens_part(h, part0, 0, CUT)

    def x_alpha(h):
        cotangent_part(h, part0, 0, CUT)
        cxa[h] = [remote(part0.at[h, :, x_at(2) * 2 + i], xa.at[h, i], xa_s.at[h, i], xa_r.at[h, i], x_peer(1 - 2 * i))
                  for i in range(2)]

    def x_direct(h):
        cxd[h] = [remote(part0.at[h, :, x_at(1 - 2 * i) * 2 + 1 - i], xd.at[h, i], xd_s.at[h, i], xd_r.at[h, i],
                         x_peer(1 - 2 * i)) for i in range(2)]

    def x_second(h, i):
        cxa[h][i].wait_recv()
        xa[h, i] = (xa[h, i].astype(F32) + part0[h, :, x_at(1 - 2 * i) * 2 + i].astype(F32)).astype(BF)
        cxc[h, i] = remote(xa.at[h, i], xc.at[h, i], xc_s.at[h, i], xc_r.at[h, i], x_peer(1 - 2 * i))

    def x_third(h):
        for cp in cxd[h] + [cxc[h, 0], cxc[h, 1]]:
            cp.wait_recv()
        for i in range(2):
            s0[h, :, i] = (part0[h, :, x * 2 + i].astype(F32) + xd[h, 1 - i].astype(F32)
                           + xc[h, i].astype(F32)).astype(BF)
        cr0[h] = remote(s0.at[h, :, 1 - yh], r0y.at[h], r0y_s.at[h], r0y_r.at[h], y_peer)

    cy1, cya, cyb = {}, {}, {}

    def y_partial(h):
        tokens_part(h, part1, CUT, G)
        cotangent_part(h, part1, CUT, G)
        cya[h], cyb[h] = {}, {}

    def y_send(h, j):
        cy1[h, j] = remote(part1.at[h, :, (1 - yh) * 4 + x_at(turn * j)], y1.at[h, j], y1_s.at[h, j], y1_r.at[h, j],
                           y_peer)

    def lap(h, kind, src, ways):
        if "a" in ways:
            cya[h][kind] = remote(src.at[:, :, pl.ds(0, PIECE)], ya.at[h, kind], ya_s.at[h, kind], ya_r.at[h, kind],
                                  x_peer(turn if kind != 1 else -turn))
        if "b" in ways:
            cyb[h][kind] = remote(src.at[:, :, pl.ds(PIECE, G - PIECE)], yb.at[h, kind], yb_s.at[h, kind],
                                  yb_r.at[h, kind], x_peer(-turn if kind != 1 else turn))

    def y_sum(h, j):
        cy1[h, j].wait_recv()
        s1[h, j] = (part1[h, :, yh * 4 + x_at(turn * j)].astype(F32) + y1[h, j].astype(F32)).astype(BF)
        if j:
            lap(h, j % 2, s1.at[h, j], ("b", "ab", "a")[j - 1])

    def y_third(h, i):
        if i == 0:
            cya[h][0].wait_recv()
            s1[h, 1, :, :, :PIECE] = (s1[h, 1, :, :, :PIECE].astype(F32) + ya[h, 0].astype(F32)).astype(BF)
            lap(h, 2, s1.at[h, 1], "a")
        else:
            cyb[h][0].wait_recv()
            s1[h, 3, :, :, PIECE:] = (s1[h, 3, :, :, PIECE:].astype(F32) + yb[h, 0].astype(F32)).astype(BF)
            lap(h, 2, s1.at[h, 3], "b")

    cg0y, cg0x, cg0f, cg1x, cg1f, cg1y = {}, {}, {}, {}, {}, {}

    def gather0(h, slot, kind):
        for i in range(2):
            cg0x[h, i, kind] = remote(all0.at[:, slot], all0.at[:, slot], g0x_s.at[h, i, kind], g0x_r.at[h, i, kind],
                                      x_peer(1 - 2 * i))

    def x_gather(h):
        cr0[h].wait_recv()
        slot = h * 8 + x * 2 + yh
        activate(s0[h, :, yh].astype(F32) + r0y[h].astype(F32), all0, slot)
        cg0y[h] = remote(all0.at[:, slot], all0.at[:, slot], g0y_s.at[h], g0y_r.at[h], y_peer)
        gather0(h, slot, 0)

    def x_gather_second(h):
        cg0y[h].wait_recv()
        gather0(h, h * 8 + x * 2 + 1 - yh, 1)

    def x_forward(h, i):
        slot = h * 8 + (x_at(-1) * 2 + yh if i == 0 else x_at(1) * 2 + 1 - yh)
        cg0x[h, i, i].wait_recv()
        cg0f[h, i] = remote(all0.at[:, slot], all0.at[:, slot], g0f_s.at[h, i], g0f_r.at[h, i], x_peer(1 - 2 * i))

    def x_done(h):
        for cp in (cg0x[h, 0, 1], cg0x[h, 1, 0], cg0f[h, 0], cg0f[h, 1]):
            cp.wait_recv()

    def to_y(h, j, slot):
        cg1y[h, j] = remote(all1.at[:, slot], all1.at[:, slot], g1y_s.at[h, j], g1y_r.at[h, j], y_peer)

    def y_gather(h):
        for cp in (cya[h][1], cya[h][2], cyb[h][1], cyb[h][2]):
            cp.wait_recv()
        mine = s1[h, 0].astype(F32)
        left = mine[:, :, :PIECE] + ya[h, 1].astype(F32) + ya[h, 2].astype(F32)
        right = mine[:, :, PIECE:] + yb[h, 1].astype(F32) + yb[h, 2].astype(F32)
        slot = h * 8 + yh * 4 + x
        activate(jnp.concatenate([left, right], axis=2), all1, slot)
        for i in range(2):
            cg1x[h, i] = remote(all1.at[:, slot], all1.at[:, slot], g1x_s.at[h, i], g1x_r.at[h, i],
                                x_peer(turn * (1 - 2 * i)))
        to_y(h, 0, slot)

    def y_forward(h, i):
        lo, width = ((0, PIECE), (PIECE, G - PIECE))[i]
        slot = h * 8 + yh * 4 + x_at(turn * (2 * i - 1))
        cg1x[h, i].wait_recv()
        piece = all1.at[:, slot, :, pl.ds(lo, width)]
        cg1f[h, i] = remote(piece, piece, g1f_s.at[h, i], g1f_r.at[h, i], x_peer(turn * (1 - 2 * i)))
        to_y(h, 3 - 2 * i, slot)

    def y_forward_last(h):
        for i in range(2):
            cg1f[h, i].wait_recv()
        to_y(h, 2, h * 8 + yh * 4 + x_at(2))

    def y_done(h):
        for j in range(4):
            cg1y[h, j].wait_recv()

    pair = {}

    def output(h, a):
        rows = slice(8 * h, 8 * h + 8)
        which = (0,) if a == 0 else (1, 2)
        left = {i: (all0[i, rows].reshape(8 * B, CUT), all1[i, rows].reshape(8 * B, G)) for i in which}
        for n in range(2):
            cols = slice(n * 512, n * 512 + 512)
            if a == 0:
                value = dot(left[0][0], dw[:CUT, cols]) + dot(left[0][1], dw[CUT:, cols])
            else:
                value = (dot_t(left[1][0], gw[cols, :CUT]) + dot_t(left[1][1], gw[cols, CUT:])
                         + dot_t(left[2][0], uw[cols, :CUT]) + dot_t(left[2][1], uw[cols, CUT:]))
            value = value.astype(BF).reshape(4, 2, B, 512)
            for core in range(2):
                pk[core, a, 4 * h:4 * h + 4, :, cols] = value[:, core]
        half = pl.ds(4 * h, 4)
        pair[h, a] = remote(pk.at[1 - k, a, half], sk.at[a, half], ks.at[h, a], kr.at[h, a], sibling)

    summed = {}

    def add_pair(h, a):
        pair[h, a].wait_recv()
        half = slice(4 * h, 4 * h + 4)
        ps[a, half] = (pk[k, a, half].astype(F32) + sk[a, half].astype(F32)).astype(BF)

    def reduce_first():
        for a in range(2):
            add_pair(0, a)
        summed["far"] = remote(ps.at[:, pl.ds(2, 2)], pz, p4s.at[0], p4r.at[0], plane_peer(2, 0))

    def reduce_first_lo():
        summed["far"].wait_recv()
        pq[...] = (ps[:, 0:2].astype(F32) + pz[...].astype(F32)).astype(BF)
        summed["lo"] = remote(pq.at[:, 1 - yl], py, p4s.at[1], p4r.at[1], lo_peer)

    def reduce_second(a):
        add_pair(1, a)
        for i, (t, dyl) in enumerate(((2, 0), (3, 0), (2, 1), (3, 1))):
            summed[a, i] = remote(ps.at[a, t * 2 + (yl + dyl) % 2], pr.at[i, a], p4s.at[2 + 4 * a + i],
                                  p4r.at[2 + 4 * a + i], plane_peer(OFFSETS[t], dyl))

    def grads(h, which):
        rows = slice(8 * h, 8 * h + 8)
        out = (gate_out, up_out, down_out)[which]

        def put(where, value):
            out[where] = value if h == 0 else out[where] + value

        for part, lo, width in ((all0, 0, CUT), (all1, CUT, G)):
            cols = slice(lo, lo + width)
            if which < 2:
                right = part[1 + which, rows].reshape(8 * B, width)
                for n in range(4):
                    feats = slice(n * 256, n * 256 + 256)
                    put((feats, cols), dot_rows(buf[0, rows, :, feats].reshape(8 * B, 256), right))
            else:
                left = part[0, rows].reshape(8 * B, width)
                for n in range(4):
                    feats = slice(n * 256, n * 256 + 256)
                    put((cols, feats), dot_rows(left, buf[1, rows, :, feats].reshape(8 * B, 256)))

    def finish():
        summed["lo"].wait_recv()
        for a, out in enumerate((mixed_out, tg_out)):
            total = pq[a, yl].astype(F32) + py[a].astype(F32)
            for i in range(4):
                summed[a, i].wait_recv()
                total = total + pr[i, a].astype(F32)
            out[...] = total

    spread_first()
    for cp in weights:
        cp.wait()
    spread_last(0)
    spread_last(1)
    ready(0, 0)
    x_tokens(0)
    ready(0, 1)
    y_partial(0)
    y_send(0, 0)
    x_alpha(0)
    spread_second(0)
    ready(1, 0)
    spread_second(1)
    y_send(0, 3)
    y_send(0, 1)
    ready(1, 1)
    y_send(0, 2)
    x_direct(0)
    x_second(0, 0)
    x_second(0, 1)
    x_tokens(1)
    y_partial(1)
    y_send(1, 1)
    x_alpha(1)
    y_sum(0, 1)
    y_sum(0, 2)
    x_direct(1)
    y_send(1, 0)
    x_third(0)
    y_sum(0, 3)
    y_third(0, 1)
    x_second(1, 0)
    y_sum(1, 1)
    x_second(1, 1)
    y_send(1, 2)
    y_third(0, 0)
    y_sum(0, 0)
    y_send(1, 3)
    x_gather(0)
    y_gather(0)
    x_gather_second(0)
    y_sum(1, 2)
    x_third(1)
    y_forward(0, 0)
    y_sum(1, 0)
    y_forward(0, 1)
    y_sum(1, 3)
    y_third(1, 0)
    y_third(1, 1)
    x_forward(0, 1)
    x_forward(0, 0)
    y_forward_last(0)
    y_gather(1)
    x_gather(1)
    x_done(0)
    y_done(0)
    output(0, 0)
    output(0, 1)
    reduce_first()
    y_forward(1, 0)
    y_forward(1, 1)
    x_gather_second(1)
    grads(0, 1)
    y_forward_last(1)
    x_forward(1, 0)
    x_forward(1, 1)
    reduce_first_lo()
    y_done(1)
    x_done(1)
    output(1, 0)
    reduce_second(0)
    output(1, 1)
    grads(0, 2)
    reduce_second(1)
    grads(0, 0)
    grads(1, 0)
    grads(1, 2)
    grads(1, 1)
    finish()
    for cp in sends:
        cp.wait_send()


def write(*refs):
    sems = refs[10]
    copies = []
    for i in range(2, 5):
        rows = refs[i].shape[0] // PARTS
        for n in range(PARTS):
            part = pl.ds(n * rows, rows)
            copies.append((refs[i].at[part], refs[5 + i].at[part]))
    copies += [(refs[i], refs[5 + i]) for i in range(2)]
    copies = [pltpu.make_async_copy(a, b, sems.at[n]) for n, (a, b) in enumerate(copies)]
    for cp in copies:
        cp.start()
    for cp in copies:
        cp.wait()


def body(tokens, gate_weight, up_weight, down_weight, cotangent):
    dma = lambda *shape: [pltpu.SemaphoreType.DMA(shape)] * 2
    vmem = lambda *shape: pltpu.VMEM(shape, BF)
    whole = pl.BlockSpec(memory_space=pltpu.HBM)
    results = pl.pallas_call(
        kernel,
        out_shape=(
            jax.ShapeDtypeStruct((B, D), F32),
            jax.ShapeDtypeStruct((B, D), F32),
            jax.ShapeDtypeStruct((D, F), F32),
            jax.ShapeDtypeStruct((D, F), F32),
            jax.ShapeDtypeStruct((F, D), F32),
        ),
        in_specs=[whole] * 5,
        out_specs=(pl.BlockSpec(memory_space=pltpu.VMEM),) * 5,
        scratch_shapes=[
            vmem(2, 16, B, D), vmem(D, F), vmem(D, F), vmem(F, D),
            vmem(2, 3, 8, B, CUT), vmem(2, 3, 8, B, G),
            vmem(2, 2, 3, B, CUT), vmem(2, 2, 3, B, CUT), vmem(2, 2, 3, B, CUT),
            vmem(2, 3, 2, B, CUT), vmem(2, 3, B, CUT),
            vmem(2, 4, 3, B, G), vmem(2, 4, 3, B, G),
            vmem(2, 3, 3, B, PIECE), vmem(2, 3, 3, B, G - PIECE),
            vmem(3, 16, B, CUT), vmem(3, 16, B, G),
            vmem(2, 2, 8, B, D), vmem(2, 8, B, D), vmem(2, 8, B, D),
            vmem(2, 2, B, D), vmem(2, 2, B, D), vmem(2, B, D), vmem(4, 2, B, D),
            pltpu.SemaphoreType.DMA((3,)), pltpu.SemaphoreType.DMA((2,)),
            *dma(2, 7), *dma(2, 8),
            *dma(2, 2), *dma(2, 2), *dma(2, 2), *dma(2), *dma(2, 4), *dma(2, 3), *dma(2, 3),
            *dma(2), *dma(2, 2, 2), *dma(2, 2), *dma(2, 2), *dma(2, 2), *dma(2, 4),
            *dma(2, 2), *dma(10),
        ],
        compiler_params=pltpu.CompilerParams(
            collective_id=0, has_side_effects=True, vmem_limit_bytes=38 * 2**20
        ),
    )(*(pltpu.with_memory_space_constraint(a, pltpu.HBM)
        for a in (tokens, cotangent, gate_weight, up_weight, down_weight)))
    return pl.pallas_call(
        write,
        out_shape=tuple(jax.ShapeDtypeStruct(r.shape, F32) for r in results),
        in_specs=[pl.BlockSpec(memory_space=pltpu.VMEM)] * 5,
        out_specs=(pl.BlockSpec(memory_space=pl.ANY),) * 5,
        scratch_shapes=[pltpu.SemaphoreType.DMA((3 * PARTS + 2,))],
        compiler_params=pltpu.CompilerParams(vmem_limit_bytes=2**20),
    )(*(pltpu.with_memory_space_constraint(r, pltpu.VMEM) for r in results))


def solution(mesh):
    placed = (
        P(("depth", "col"), "row"),
        P("row", ("col", "depth")),
        P("row", ("col", "depth")),
        P(("col", "depth"), "row"),
        P(("depth", "col"), "row"),
    )
    return jax.shard_map(
        body,
        mesh=mesh,
        in_specs=placed,
        out_specs=(
            P(("depth", "col"), "row"),
            P(("depth", "col"), "row"),
            P("row", ("col", "depth")),
            P("row", ("col", "depth")),
            P(("col", "depth"), "row"),
        ),
        check_vma=False,
    )
```
